256 devices in a mesh: pair: 16 (over z_hi, y, core), ga: 16 (over z_lo, x).
Axes of the slice: x: 4, y: 4, z: 8 (z_hi: 2, z_lo: 4; z = z_hi * 4 + z_lo), core: 2. Of those that a mesh axis runs over, the one named last changes fastest.
Arguments:
- orbitals: bfloat16 [2, 8, 96, 18432], P(None, None, 'ga'), may hold values from -6 to 6
- owner: int32 [2, 8], replicated, may hold values from 0 to 7, each once within a row
- pair_list: int32 [64, 2], P('pair'), may hold values from 0 to 7
- valence_energy: float32 [8], replicated, may hold values from -12 to -2
- conduction_energy: float32 [8], replicated, may hold values from 0.5 to 6
- sphere_index: int32 [4096], replicated, may hold values from 0 to 1769471, as said below
Outputs:
- polarizability: float32 [2, 4096, 4096], P(None, 'ga', 'pair')
The draws below stay inside these ranges and needn't reach their ends.
Inputs may be any that keep to these rules, and one draw needn't show every extreme that they name: `owner`: each row is a permutation of the 8 slots. `sphere_index`: 4096 distinct positions x * 96 * 192 + y * 192 + z whose signed frequencies f (index, less the grid length from the upper half on) give the smallest values of 4 fx^2 + 4 fy^2 + fz^2, in rising order of that value, equal values in a random order.
All inputs are finite; a program needn't handle non-finite values.
Results may differ from the reference program's by a relative error of at most 0.0003.
Values sent between devices are 32-bit elements; how exact they have to be, the bound alone decides.
A program may use at most 256 MiB of HBM per device.

```python
import math
import jax
import jax.numpy as jnp
from jax import lax

NX = 96
NY = 96
NZ = 192
NG = 4096
NB = 8
PAIRS = 64


def draw_sphere_index(key, part):
    key = jax.random.fold_in(key, 11)
    flattened = jnp.arange(NX * NY * NZ, dtype=jnp.int32)
    index_x = flattened // (NY * NZ)
    index_y = flattened // NZ % NY
    index_z = flattened % NZ
    freq_x = jnp.where(2 * index_x >= NX, index_x - NX, index_x)
    freq_y = jnp.where(2 * index_y >= NY, index_y - NY, index_y)
    freq_z = jnp.where(2 * index_z >= NZ, index_z - NZ, index_z)
    shell = 4 * freq_x * freq_x + 4 * freq_y * freq_y + freq_z * freq_z
    tiebreak = jax.random.randint(key, (NX * NY * NZ,), 0, 2048, dtype=jnp.int32)
    ranking = jnp.argsort(shell * 2048 + tiebreak, stable=True)
    return ranking[:NG].astype(jnp.int32)


def set_ends(result, key, least, largest):
    longest = result.shape.index(max(result.shape))
    spots = []
    for shift in (0, 1):
        where = [jax.random.randint(jax.random.fold_in(key, axis), (), 0, length) for axis, length in enumerate(result.shape)]
        where[longest] = (where[longest] + shift) % result.shape[longest]
        spots.append(tuple(where))
    return result.at[spots[0]].set(least).at[spots[1]].set(largest)


def shard_levels(own_key, shape, cuts, least, high):
    level, own = 1.0, jax.random.fold_in(own_key, 6)
    for position, shards_of in cuts:
        draws = jnp.exp(jax.random.uniform(jax.random.fold_in(own, position), (shards_of,), jnp.float32, least / len(cuts), high / len(cuts)))
        level = level * jnp.repeat(draws, shape[position] // shards_of).reshape([-1 if axis == position else 1 for axis in range(len(shape))])
    return level


def centred(rng, extent, spread, reach, cuts=(), kind=jnp.bfloat16):
    gain = shard_levels(rng, extent, cuts, -0.22, 0.18) if cuts else 1.0
    values = jax.random.normal(rng, extent, jnp.float32) * spread * gain
    return jnp.minimum(jnp.maximum(values, -reach), reach).astype(kind)


def setup_inputs(seed: int = 0) -> dict:
    key_of = jax.random.split(jax.random.key(seed), 7)
    orbitals = centred(key_of[0], (2, NB, NX, NY * NZ), 1.0, 6.0, ((2, 16),))
    owner = jax.vmap(lambda own: jax.random.permutation(own, NB))(jax.random.split(key_of[1], 2)).reshape((2, NB)).astype(jnp.int32)
    pair_list = set_ends(jax.random.randint(key_of[2], (PAIRS, 2), 0, NB), jax.random.fold_in(key_of[2], 1), 0, NB - 1).astype(jnp.int32)
    valence_energy = jnp.clip(jax.random.uniform(key_of[3], (NB,), jnp.float32, -12.0, -2.0), -12.0, -2.0)
    conduction_energy = jnp.clip(jax.random.uniform(key_of[4], (NB,), jnp.float32, 0.5, 6.0), 0.5, 6.0)
    sphere_index = draw_sphere_index(jax.random.fold_in(key_of[6], 71), 0)
    return {"orbitals": orbitals, "owner": owner, "pair_list": pair_list, "valence_energy": valence_energy, "conduction_energy": conduction_energy, "sphere_index": sphere_index}


def reference(orbitals, owner, pair_list, valence_energy, conduction_energy, sphere_index):
    valence = pair_list[:, 0]
    conduction = pair_list[:, 1]
    slot_val = owner[0][valence]
    slot_con = owner[1][conduction]
    weights = 2.0 / (valence_energy[valence] - conduction_energy[conduction])

    def transform(slot_pair):
        val_grid = lax.dynamic_index_in_dim(orbitals[0], slot_pair[0], 0, keepdims=False)
        con_grid = lax.dynamic_index_in_dim(orbitals[1], slot_pair[1], 0, keepdims=False)
        product = val_grid.astype(jnp.float32) * con_grid.astype(jnp.float32)
        spectrum = jnp.fft.fftn(product.reshape(NX, NY, NZ)).reshape(-1)
        picked = jnp.take(spectrum, sphere_index)
        return jnp.stack([jnp.real(picked), jnp.imag(picked)])
    coefficient = lax.map(transform, (slot_val, slot_con)) * (1.0 / math.sqrt(NX * NY * NZ))
    weighted = coefficient * weights[:, None, None]
    highest = lax.Precision.HIGHEST
    real_part = jnp.dot(weighted[:, 0].T, coefficient[:, 0], precision=highest, preferred_element_type=jnp.float32)
    real_part = real_part + jnp.dot(weighted[:, 1].T, coefficient[:, 1], precision=highest, preferred_element_type=jnp.float32)
    imag_part = jnp.dot(weighted[:, 1].T, coefficient[:, 0], precision=highest, preferred_element_type=jnp.float32)
    imag_part = imag_part - jnp.dot(weighted[:, 0].T, coefficient[:, 1], precision=highest, preferred_element_type=jnp.float32)
    factor = 1.0 / math.sqrt(PAIRS)
    return jnp.stack([real_part, imag_part]) * factor
```

```python
import math

import jax
import jax.numpy as jnp
import ml_dtypes
import numpy as np
from jax import lax
from jax.experimental import pallas as pl
from jax.experimental.pallas import tpu as pltpu
from jax.sharding import PartitionSpec as P

NX = 96
NY = 96
NZ = 192
NG = 4096
PAIRS = 64
GROUPS = 16
PLANES = NX // GROUPS
HERE = PAIRS // GROUPS
ROWS = PLANES * HERE
STEP = 4
CHUNKS = NY // STEP
WIDE = STEP * NZ
KY = 8
KZ = 16
KX = 7
BLOCK = NG // GROUPS
LOADS = 4
MESH = pl.DeviceIdType.MESH
OFFSETS = sorted(((e, d) for e in range(4) for d in range(4)), key=lambda o: -(o[0] + min(o[1], 4 - o[1])))


def split(table):
    high = table.astype(ml_dtypes.bfloat16)
    low = (table - high.astype(np.float64)).astype(ml_dtypes.bfloat16)
    return high, low


def table_along_z():
    angle = 2 * math.pi * (np.arange(NZ)[:, None] * np.arange(KZ)[None, :] % NZ) / NZ
    table = np.zeros((STEP, NZ, STEP, 2, KZ))
    for r in range(STEP):
        table[r, :, r, 0] = np.cos(angle)
        table[r, :, r, 1] = -np.sin(angle)
    return np.concatenate(split(table.reshape(WIDE, STEP * 2 * KZ)), 1)


def twiddles():
    angle = 2 * math.pi * np.arange(KY)[:, None] * np.arange(STEP)[None, :] / NY
    angle = np.repeat(angle, 2 * KZ, 1)
    return np.concatenate([np.cos(angle), np.sin(angle)]).astype(np.float32)


def table_along_x():
    table = np.zeros((GROUPS, 2, PLANES, HERE, 256))
    for j in range(GROUPS):
        for x in range(PLANES):
            for f in range(-KX, KX + 1):
                angle = 2 * math.pi * (f * (PLANES * j + x) % NX) / NX
                table[j, 0, x, :, 16 + f + KX] = math.cos(angle)
                table[j, 1, x, :, 16 + f + KX] = math.sin(angle)
    high, low = split(table.reshape(GROUPS, 2 * ROWS, 256))
    return np.concatenate([high, low], 1)


def halves(value):
    high = value.astype(jnp.bfloat16)
    return high, (value - high.astype(jnp.float32)).astype(jnp.bfloat16)


def dot(left, right):
    return jnp.dot(left, right, preferred_element_type=jnp.float32)


def rem(value, size):
    return lax.rem(value, size)


def coefficients_kernel(
    owner_in, pairs_in, energy_v_in, energy_c_in, sphere_in, orbitals, table_z, table_y, table_x, rows, cols,
    owner, pairs, energy_v, energy_c, sphere, orb, tz, ty, tx, high_ref, low_ref, along_z, hot, left, part, landed, total,
    sems, send1, recv1, send_col, recv_col, send_row, recv_row, send_fc, recv_fc, send_fr, recv_fr,
):
    i, j = lax.axis_index("pair"), lax.axis_index("ga")
    zh, y, core = i // 8, rem(i // 2, 4), rem(i, 2)
    zl, x = j // 4, rem(j, 4)
    sibling = i + 1 - 2 * core

    def pair_at(zh, y, core):
        return zh * 8 + rem(y, 4) * 2 + core

    def ga_at(zl, x):
        return rem(zl, 4) * 4 + rem(x, 4)

    mine = ga_at(zl + 2, x + 4 - y)
    own = mine == i
    col_y = rem(x + 4 - rem(i, 4), 4)

    moves = (
        (owner_in, owner), (pairs_in, pairs), (energy_v_in, energy_v), (energy_c_in, energy_c), (sphere_in, sphere),
        (table_z, tz), (table_x.at[j], tx), (table_y, ty),
    )
    copies = [pltpu.make_async_copy(source, target, sems.at[LOADS + n]) for n, (source, target) in enumerate(moves)]
    loads = []
    span = CHUNKS // LOADS * WIDE
    for n in range(LOADS):
        lanes = pl.ds(n * span, span)
        loads.append(pltpu.make_async_copy(orbitals.at[:, lanes], orb.at[:, lanes], sems.at[n]))
    for copy in copies[4:5] + loads[:1] + copies[:4] + copies[5:6] + loads[1:] + copies[6:]:
        copy.start()

    barrier = pltpu.get_barrier_semaphore()

    def greet(device):
        pl.semaphore_signal(barrier, inc=1, device_id=device, device_id_type=MESH)

    turn = jnp.where(zl < 2, 1, 3)
    for e, d in OFFSETS[:-1]:
        greet((i, ga_at(zl + turn * e, x + d)))
    across = ga_at(jnp.where(zl < 2, 3, 0), x)
    for d in (2, 1, 3, 0):
        greet((pair_at(1 - zh, y + d, core), across))
    greet((pair_at(1 - zh, col_y, 1 - core), across))
    for d in (2, 1, 3):
        greet((pair_at(zh, y + d, core), j))
    greet((pair_at(zh, col_y, 1 - core), j))
    greet((sibling, j))
    side = jnp.where(rem(zl, 3) == 0, 1, 0)
    even = 1 - rem(x + 4 - (1 - core) + y, 2)
    greeted = (GROUPS - 1) + 4 + 8 * side + even * (2 + 4 * side)

    copies[4].wait()
    position = sphere[...]
    column = lax.shift_right_logical(lax.shift_right_logical(position, 6) * 43691, 17)
    index_z = position - column * NZ
    index_x = lax.shift_right_logical(lax.shift_right_logical(column, 5) * 43691, 17)
    index_y = column - index_x * NY
    freq_x = jnp.where(index_x >= NX // 2, index_x - NX, index_x)
    freq_y = jnp.where(index_y >= NY // 2, index_y - NY, index_y)
    freq_z = jnp.where(index_z >= NZ // 2, index_z - NZ, index_z)
    flip = freq_z < 0
    freq_x = jnp.where(flip, -freq_x, freq_x) + KX
    freq_y = jnp.where(flip, -freq_y, freq_y)
    mode = jnp.abs(freq_y) * 32 + jnp.where(freq_y < 0, 16, 0) + jnp.abs(freq_z)
    sign = jnp.where(flip, -1.0, 1.0)
    row = lax.broadcasted_iota(jnp.int32, (256, BLOCK), 0)
    for b in range(GROUPS):
        lanes = slice(b * BLOCK, (b + 1) * BLOCK)
        hot[b, :256] = jnp.where(row == mode[:, lanes], 1.0, 0.0).astype(jnp.bfloat16)
        hot[b, 16:32] = jnp.where(row[:16] == freq_x[:, lanes], 1.0, 0.0).astype(jnp.bfloat16)
        hot[b, 256:] = jnp.broadcast_to(sign[:, lanes], (16, BLOCK)).astype(jnp.bfloat16)

    for copy in copies[:4]:
        copy.wait()
    place = rem(lax.broadcasted_iota(jnp.int32, (8, WIDE), 0), HERE)
    slot_v = jnp.zeros((8, WIDE), jnp.int32)
    slot_c = jnp.zeros((8, WIDE), jnp.int32)
    gap = jnp.zeros((8, BLOCK), jnp.float32)
    for p in range(HERE):
        v, c = pairs[0, p], pairs[1, p]
        slot_v = jnp.where(place == p, owner[0, v], slot_v)
        slot_c = jnp.where(place == p, owner[1, c], slot_c)
        gap = jnp.where(place[:, :BLOCK] == p, energy_c[c] - energy_v[v], gap)
    scale = jnp.sqrt(2.0 / gap) * (1.0 / math.sqrt(NX * NY * NZ * math.sqrt(PAIRS)))

    upper = lax.broadcasted_iota(jnp.int32, (8, WIDE), 0) < HERE

    def pick(value, slots):
        return jnp.take_along_axis(value, slots, axis=0, mode="promise_in_bounds")

    copies[5].wait()
    group = CHUNKS // LOADS
    for n in range(LOADS):
        loads[n].wait()

        @pl.loop(n * group // 2, (n + 1) * group // 2, unroll=True)
        def _(u):
            values = []
            for s in range(2):
                lanes = pl.ds(pl.multiple_of((2 * u + s) * WIDE, 128), WIDE)
                for a in range(PLANES // 2):
                    val = orb[16 * a : 16 * a + 16, lanes].astype(jnp.float32)
                    con = orb[48 + 16 * a : 64 + 16 * a, lanes].astype(jnp.float32)
                    first = pick(val[:8], slot_v) * pick(con[:8], slot_c)
                    second = pick(val[8:], slot_v) * pick(con[8:], slot_c)
                    values.append(jnp.where(upper, first, second))
            high, low = halves(jnp.concatenate(values, 0))
            here = pl.ds(pl.multiple_of(u * 2 * ROWS, 16), 2 * ROWS)
            high_ref[here] = high
            low_ref[here] = low

        here = slice(n * group * ROWS, (n + 1) * group * ROWS)
        result = dot(high_ref[here], tz[...]) + dot(low_ref[here], tz[...])
        result = result[:, :128] + result[:, 128:]
        along_z[n * group : (n + 1) * group] = result.reshape(group, ROWS, 128)

    for copy in copies[6:]:
        copy.wait()
    lane = lax.broadcasted_iota(jnp.int32, (8, 128), 1)
    real_lane = rem(lane, 2 * KZ) < KZ
    turn_sign = jnp.where(real_lane, 1.0, -1.0)
    modes = [[], []]
    for a in range(ROWS // 8):
        here = slice(a * 8, a * 8 + 8)
        first, middle = along_z[0, here], along_z[CHUNKS // 2, here]
        even, odd = [], []
        for t in range(1, CHUNKS // 2):
            one, other = along_z[t, here], along_z[CHUNKS - t, here]
            even.append(one + other)
            odd.append(one - other)
        placed = [[None, None], [None, None]]
        for k in range(KY):
            total_cos = first + middle if k % 2 == 0 else first - middle
            total_sin = None
            for t in range(1, CHUNKS // 2):
                angle = 2 * math.pi * (k * t % CHUNKS) / CHUNKS
                total_cos = total_cos + even[t - 1] * math.cos(angle)
                term = odd[t - 1] * math.sin(angle)
                total_sin = term if total_sin is None else total_sin + term
            cosine, sine = ty[k : k + 1], ty[KY + k : KY + k + 1]
            same = cosine * total_cos - sine * total_sin
            cross = sine * total_cos + cosine * total_sin
            for shift in (2 * KZ, 4 * KZ):
                same = same + pltpu.roll(same, shift, 1)
                cross = cross + pltpu.roll(cross, shift, 1)
            cross = pltpu.roll(cross, KZ, 1) * turn_sign
            plus, minus = same + cross, same - cross
            real = jnp.where(real_lane, plus, pltpu.roll(minus, KZ, 1))
            imag = jnp.where(real_lane, pltpu.roll(plus, KZ, 1), minus)
            if k == 0:
                real, imag = jnp.where(real_lane, real, 0.0), jnp.where(real_lane, imag, 0.0)
            spot = lane // (2 * KZ) == k % 4
            for c, value in enumerate((real, imag)):
                old = placed[c][k // 4]
                placed[c][k // 4] = value if old is None else jnp.where(spot, value, old)
        for c in range(2):
            modes[c].append(jnp.concatenate(placed[c], 1))
    high, low = halves(jnp.concatenate(modes[0] + modes[1], 0))
    left[: 2 * ROWS] = high
    left[2 * ROWS : 4 * ROWS] = low
    left[4 * ROWS :] = tx[...]

    pl.semaphore_wait(barrier, greeted)
    upper = upper[:, :BLOCK]

    def to_group(n, slot, peer):
        return pltpu.make_async_remote_copy(
            part.at[n], landed.at[slot], send1.at[n], recv1.at[slot], device_id=(i, peer), device_id_type=MESH
        )

    sent = []
    for n, (e, d) in enumerate(OFFSETS):
        peer = ga_at(zl + turn * e, x + d)
        block = ga_at(zl + turn * e + 2, x + d + 4 - y)
        picked = dot(left[...], hot[block, :256])
        real = imag = jnp.zeros((8, BLOCK), jnp.float32)
        for a in range(ROWS // 8):
            re, im, cosine, sine = [
                picked[s * ROWS + a * 8 : s * ROWS + a * 8 + 8]
                + picked[s * ROWS + lag * ROWS + a * 8 : s * ROWS + lag * ROWS + a * 8 + 8]
                for s, lag in ((0, 2), (1, 2), (4, 2), (5, 2))
            ]
            real = real + cosine * re + sine * im
            imag = imag + cosine * im - sine * re
        imag = imag * hot[block, 256:].astype(jnp.float32)[:8]
        real = real + pltpu.roll(real, HERE, 0)
        imag = imag + pltpu.roll(imag, HERE, 0)
        part[n] = jnp.where(upper, real, imag) * scale
        if n < GROUPS - 1:
            copy = to_group(n, j, peer)
            copy.start()
            sent.append(copy)

    value = part[GROUPS - 1]
    for n, (e, d) in reversed(list(enumerate(OFFSETS[:-1]))):
        peer = ga_at(zl + turn * e, x + d)
        to_group(n, peer, peer).wait_recv()
        value = value + landed[peer]
    total[...] = value

    def col_slot(zh, y, core):
        return y * 4 + zh * 2 + core

    def row_slot(zh, y, core):
        return core * 8 + y * 2 + zh

    def col_copy(n, to_z, h, s):
        return pltpu.make_async_remote_copy(
            total, cols.at[s], send_col.at[n], recv_col.at[h], device_id=(mine, ga_at(to_z, x)), device_id_type=MESH
        )

    my_col = col_slot(zh, y, core)
    lift = jnp.where(mine // 8 == zh, 2, 0)

    @pl.when(own)
    def _():
        cols[my_col] = total[...]

    for n, d in enumerate((0, 1, 3, 2)):
        to_z = rem(zl + lift + d, 4)

        @pl.when(jnp.logical_not(jnp.logical_and(own, to_z == zl)))
        def _():
            col_copy(n, to_z, zh * 2 + core, my_col).start()

    def row_copy(n, to_h, to_y, h, s):
        return pltpu.make_async_remote_copy(
            total, rows.at[s], send_row.at[n], recv_row.at[h],
            device_id=(pair_at(to_h, to_y, core), mine), device_id_type=MESH,
        )

    my_row = row_slot(zh, y, core)
    targets = [(h, d) for d in (2, 1, 3, 0) for h in range(2)]
    for n, (h, d) in enumerate(targets):
        row_copy(n, h, y + d, y * 2 + zh, my_row).start()

    def pass_col(n, d, slot, sem):
        two = cols.at[pl.ds(slot, 2)]
        return pltpu.make_async_remote_copy(
            two, two, send_fc.at[n], recv_fc.at[sem], device_id=(i, ga_at(zl, x + d)), device_id_type=MESH
        )

    for step in range(2):
        h = zh if step == 0 else 1 - zh
        for c in range(2):
            self_sent = jnp.logical_and(own, jnp.logical_and(h == zh, core == c))

            @pl.when(jnp.logical_not(self_sent))
            def _():
                col_copy(0, zl, h * 2 + c, col_slot(h, col_y, c)).wait_recv()

        for n, d in enumerate((2, 1, 3)):
            pass_col(step * 3 + n, d, col_slot(h, col_y, 0), col_y * 2 + h).start()

    def pass_row(n, y, c):
        two = rows.at[pl.ds(row_slot(0, y, c), 2)]
        return pltpu.make_async_remote_copy(
            two, two, send_fr.at[n], recv_fr.at[y], device_id=(sibling, j), device_id_type=MESH
        )

    for n, d in enumerate((0, 1, 3, 2)):
        from_y = rem(y + d, 4)
        for h in range(2):
            row_copy(0, h, from_y, from_y * 2 + h, row_slot(h, from_y, core)).wait_recv()
        pass_row(n, from_y, core).start()

    for copy in sent:
        copy.wait_send()
    for n, d in enumerate((0, 1, 3, 2)):
        to_z = rem(zl + lift + d, 4)

        @pl.when(jnp.logical_not(jnp.logical_and(own, to_z == zl)))
        def _():
            col_copy(n, to_z, zh * 2 + core, my_col).wait_send()

    for n, (h, d) in enumerate(targets):
        row_copy(n, h, y + d, y * 2 + zh, my_row).wait_send()
    for n, d in enumerate((0, 1, 3, 2)):
        from_y = rem(y + d, 4)
        pass_row(n, from_y, core).wait_send()
        pass_row(n, from_y, 1 - core).wait_recv()
    for step in range(2):
        h = zh if step == 0 else 1 - zh
        for n, d in enumerate((2, 1, 3)):
            pass_col(step * 3 + n, d, col_slot(h, col_y, 0), col_y * 2 + h).wait_send()
            from_y = rem(col_y + d, 4)
            pass_col(0, d, col_slot(h, from_y, 0), from_y * 2 + h).wait_recv()


def coefficients(owner, pairs, energy_v, energy_c, sphere, orbitals):
    vmem = pl.BlockSpec(memory_space=pltpu.VMEM)
    hbm = pl.BlockSpec(memory_space=pl.ANY)
    points = NY * NZ
    block = jax.ShapeDtypeStruct((GROUPS, 8, BLOCK), jnp.float32)
    dma = pltpu.SemaphoreType.DMA
    return pl.pallas_call(
        coefficients_kernel,
        out_shape=(block, block),
        in_specs=[hbm] * 9,
        out_specs=(vmem, vmem),
        scratch_shapes=[
            pltpu.SMEM((2, 8), jnp.int32),
            pltpu.SMEM((2, HERE), jnp.int32),
            pltpu.SMEM((8,), jnp.float32),
            pltpu.SMEM((8,), jnp.float32),
            pltpu.VMEM((1, NG), jnp.int32),
            pltpu.VMEM((16 * PLANES, points), jnp.bfloat16),
            pltpu.VMEM((WIDE, 256), jnp.bfloat16),
            pltpu.VMEM((2 * KY, 128), jnp.float32),
            pltpu.VMEM((4 * ROWS, 256), jnp.bfloat16),
            pltpu.VMEM((CHUNKS * ROWS, WIDE), jnp.bfloat16),
            pltpu.VMEM((CHUNKS * ROWS, WIDE), jnp.bfloat16),
            pltpu.VMEM((CHUNKS, ROWS, 128), jnp.float32),
            pltpu.VMEM((GROUPS, 256 + 16, BLOCK), jnp.bfloat16),
            pltpu.VMEM((8 * ROWS, 256), jnp.bfloat16),
            pltpu.VMEM((GROUPS, 8, BLOCK), jnp.float32),
            pltpu.VMEM((GROUPS, 8, BLOCK), jnp.float32),
            pltpu.VMEM((8, BLOCK), jnp.float32),
            dma((LOADS + 8,)), dma((GROUPS,)), dma((GROUPS,)), dma((4,)), dma((4,)), dma((8,)), dma((8,)),
            dma((6,)), dma((8,)), dma((4,)), dma((4,)),
        ],
        compiler_params=pltpu.CompilerParams(
            collective_id=0, has_side_effects=True, vmem_limit_bytes=56 * 1024 * 1024
        ),
        name="coefficients",
    )(
        owner, pairs.T, energy_v, energy_c, sphere.reshape(1, NG),
        orbitals.transpose(0, 2, 1, 3).reshape(16 * PLANES, points),
        jnp.asarray(table_along_z()), jnp.asarray(twiddles()), jnp.asarray(table_along_x()),
    )


def outer_kernel(rows, cols, out, result, sems):
    order = [c * 8 + y * 2 + h for y in range(4) for h in range(2) for c in range(2)]
    left = jnp.concatenate([rows[n] for n in order], 0)
    left_high, left_low = halves(left)
    left = jnp.concatenate([left_high, left_high, left_low], 0)
    blocks = -cols[...]
    swapped = jnp.concatenate([-blocks[:, HERE:], blocks[:, :HERE]], 1)
    right = jnp.concatenate([v.reshape(PAIRS * 2, BLOCK) for v in (blocks, swapped)], 1)
    right_high, right_low = halves(right)
    right = jnp.concatenate([right_high, right_low, right_high], 0)
    turned = left.T
    copies = []
    for n in range(2):
        here = pl.ds(n * 128, 128)
        value = dot(turned[n * 128 : n * 128 + 128], right)
        result[0, here] = value[:, :BLOCK]
        result[1, here] = value[:, BLOCK:]
        copies.append(pltpu.make_async_copy(result.at[:, here], out.at[:, here], sems.at[n]))
        copies[-1].start()
    for copy in copies:
        copy.wait()


def outer(rows, cols):
    vmem = pl.BlockSpec(memory_space=pltpu.VMEM)
    return pl.pallas_call(
        outer_kernel,
        out_shape=jax.ShapeDtypeStruct((2, BLOCK, BLOCK), jnp.float32),
        in_specs=[vmem, vmem],
        out_specs=pl.BlockSpec(memory_space=pl.ANY),
        scratch_shapes=[pltpu.VMEM((2, BLOCK, BLOCK), jnp.float32), pltpu.SemaphoreType.DMA((2,))],
        name="outer",
    )(rows, cols)


def per_device(orbitals, owner, pair_list, valence_energy, conduction_energy, sphere_index):
    rows, cols = coefficients(owner, pair_list, valence_energy, conduction_energy, sphere_index, orbitals)
    return outer(rows, cols)


def solution(mesh):
    return jax.shard_map(
        per_device,
        mesh=mesh,
        in_specs=(P(None, None, "ga", None), P(), P("pair", None), P(), P(), P()),
        out_specs=P(None, "ga", "pair"),
        check_vma=False,
    )
```

```python
import math

import jax
import jax.numpy as jnp
import ml_dtypes
import numpy as np
from jax import lax
from jax.experimental import pallas as pl
from jax.experimental.pallas import tpu as pltpu
from jax.sharding import PartitionSpec as P

NX = 96
NY = 96
NZ = 192
NG = 4096
PAIRS = 64
GROUPS = 16
PLANES = NX // GROUPS
HERE = PAIRS // GROUPS
ROWS = PLANES * HERE
STEP = 4
CHUNKS = NY // STEP
WIDE = STEP * NZ
KY = 8
KZ = 16
KX = 7
BLOCK = NG // GROUPS
LOADS = 4
MESH = pl.DeviceIdType.MESH
OFFSETS = sorted(((e, d) for e in range(4) for d in range(4)), key=lambda o: -(o[0] + min(o[1], 4 - o[1])))


def split(table):
    high = table.astype(ml_dtypes.bfloat16)
    low = (table - high.astype(np.float64)).astype(ml_dtypes.bfloat16)
    return high, low


def table_along_z():
    angle = 2 * math.pi * (np.arange(NZ)[:, None] * np.arange(KZ)[None, :] % NZ) / NZ
    table = np.zeros((STEP, NZ, STEP, 2, KZ))
    for r in range(STEP):
        table[r, :, r, 0] = np.cos(angle)
        table[r, :, r, 1] = -np.sin(angle)
    return np.concatenate(split(table.reshape(WIDE, STEP * 2 * KZ)), 1)


def twiddles():
    angle = 2 * math.pi * np.arange(KY)[:, None] * np.arange(STEP)[None, :] / NY
    angle = np.repeat(angle, 2 * KZ, 1)
    return np.concatenate([np.cos(angle), np.sin(angle)]).astype(np.float32)


def table_along_x():
    table = np.zeros((GROUPS, 2, PLANES, HERE, 256))
    for j in range(GROUPS):
        for x in range(PLANES):
            for f in range(-KX, KX + 1):
                angle = 2 * math.pi * (f * (PLANES * j + x) % NX) / NX
                table[j, 0, x, :, 16 + f + KX] = math.cos(angle)
                table[j, 1, x, :, 16 + f + KX] = math.sin(angle)
    high, low = split(table.reshape(GROUPS, 2 * ROWS, 256))
    return np.concatenate([high, low], 1)


def halves(value):
    high = value.astype(jnp.bfloat16)
    return high, (value - high.astype(jnp.float32)).astype(jnp.bfloat16)


def dot(left, right):
    return jnp.dot(left, right, preferred_element_type=jnp.float32)


def rem(value, size):
    return lax.rem(value, size)


def coefficients_kernel(
    owner_in, pairs_in, energy_v_in, energy_c_in, sphere_in, orbitals, table_z, table_y, table_x, out,
    owner, pairs, energy_v, energy_c, sphere, orb, tz, ty, tx, high_ref, low_ref, along_z, hot, left, part, landed, total,
    rows, cols, sems, send1, recv1, send_col, recv_col, send_row, recv_row, send_fc, recv_fc, send_fr, recv_fr,
):
    i, j = lax.axis_index("pair"), lax.axis_index("ga")
    zh, y, core = i // 8, rem(i // 2, 4), rem(i, 2)
    zl, x = j // 4, rem(j, 4)
    sibling = i + 1 - 2 * core

    def pair_at(zh, y, core):
        return zh * 8 + rem(y, 4) * 2 + core

    def ga_at(zl, x):
        return rem(zl, 4) * 4 + rem(x, 4)

    mine = ga_at(zl + 2, x + 4 - y)
    own = mine == i
    col_y = rem(x + 4 - rem(i, 4), 4)

    moves = (
        (owner_in, owner), (pairs_in, pairs), (energy_v_in, energy_v), (energy_c_in, energy_c), (sphere_in, sphere),
        (table_z, tz), (table_x.at[j], tx), (table_y, ty),
    )
    copies = [pltpu.make_async_copy(source, target, sems.at[LOADS + n]) for n, (source, target) in enumerate(moves)]
    loads = []
    span = CHUNKS // LOADS * WIDE
    for n in range(LOADS):
        lanes = pl.ds(n * span, span)
        loads.append(pltpu.make_async_copy(orbitals.at[:, lanes], orb.at[:, lanes], sems.at[n]))
    for copy in copies[4:5] + loads[:1] + copies[:4] + copies[5:6] + loads[1:] + copies[6:]:
        copy.start()

    barrier = pltpu.get_barrier_semaphore()

    def greet(device):
        pl.semaphore_signal(barrier, inc=1, device_id=device, device_id_type=MESH)

    turn = jnp.where(zl < 2, 1, 3)
    for e, d in OFFSETS[:-1]:
        greet((i, ga_at(zl + turn * e, x + d)))
    across = ga_at(jnp.where(zl < 2, 3, 0), x)
    for d in (2, 1, 3, 0):
        greet((pair_at(1 - zh, y + d, core), across))
    greet((pair_at(1 - zh, col_y, 1 - core), across))
    for d in (2, 1, 3):
        greet((pair_at(zh, y + d, core), j))
    greet((pair_at(zh, col_y, 1 - core), j))
    greet((sibling, j))
    side = jnp.where(rem(zl, 3) == 0, 1, 0)
    even = 1 - rem(x + 4 - (1 - core) + y, 2)
    greeted = (GROUPS - 1) + 4 + 8 * side + even * (2 + 4 * side)

    copies[4].wait()
    position = sphere[...]
    column = lax.shift_right_logical(lax.shift_right_logical(position, 6) * 43691, 17)
    index_z = position - column * NZ
    index_x = lax.shift_right_logical(lax.shift_right_logical(column, 5) * 43691, 17)
    index_y = column - index_x * NY
    freq_x = jnp.where(index_x >= NX // 2, index_x - NX, index_x)
    freq_y = jnp.where(index_y >= NY // 2, index_y - NY, index_y)
    freq_z = jnp.where(index_z >= NZ // 2, index_z - NZ, index_z)
    flip = freq_z < 0
    freq_x = jnp.where(flip, -freq_x, freq_x) + KX
    freq_y = jnp.where(flip, -freq_y, freq_y)
    mode = jnp.abs(freq_y) * 32 + jnp.where(freq_y < 0, 16, 0) + jnp.abs(freq_z)
    sign = jnp.where(flip, -1.0, 1.0)
    row = lax.broadcasted_iota(jnp.int32, (256, BLOCK), 0)
    for b in range(GROUPS):
        lanes = slice(b * BLOCK, (b + 1) * BLOCK)
        hot[b, :256] = jnp.where(row == mode[:, lanes], 1.0, 0.0).astype(jnp.bfloat16)
        hot[b, 16:32] = jnp.where(row[:16] == freq_x[:, lanes], 1.0, 0.0).astype(jnp.bfloat16)
        hot[b, 256:] = jnp.broadcast_to(sign[:, lanes], (16, BLOCK)).astype(jnp.bfloat16)

    for copy in copies[:4]:
        copy.wait()
    place = rem(lax.broadcasted_iota(jnp.int32, (8, WIDE), 0), HERE)
    slot_v = jnp.zeros((8, WIDE), jnp.int32)
    slot_c = jnp.zeros((8, WIDE), jnp.int32)
    gap = jnp.zeros((8, BLOCK), jnp.float32)
    for p in range(HERE):
        v, c = pairs[0, p], pairs[1, p]
        slot_v = jnp.where(place == p, owner[0, v], slot_v)
        slot_c = jnp.where(place == p, owner[1, c], slot_c)
        gap = jnp.where(place[:, :BLOCK] == p, energy_c[c] - energy_v[v], gap)
    scale = jnp.sqrt(2.0 / gap) * (1.0 / math.sqrt(NX * NY * NZ * math.sqrt(PAIRS)))

    upper = lax.broadcasted_iota(jnp.int32, (8, WIDE), 0) < HERE

    def pick(value, slots):
        return jnp.take_along_axis(value, slots, axis=0, mode="promise_in_bounds")

    copies[5].wait()
    group = CHUNKS // LOADS
    for n in range(LOADS):
        loads[n].wait()

        @pl.loop(n * group // 2, (n + 1) * group // 2, unroll=True)
        def _(u):
            values = []
            for s in range(2):
                lanes = pl.ds(pl.multiple_of((2 * u + s) * WIDE, 128), WIDE)
                for a in range(PLANES // 2):
                    val = orb[16 * a : 16 * a + 16, lanes].astype(jnp.float32)
                    con = orb[48 + 16 * a : 64 + 16 * a, lanes].astype(jnp.float32)
                    first = pick(val[:8], slot_v) * pick(con[:8], slot_c)
                    second = pick(val[8:], slot_v) * pick(con[8:], slot_c)
                    values.append(jnp.where(upper, first, second))
            high, low = halves(jnp.concatenate(values, 0))
            here = pl.ds(pl.multiple_of(u * 2 * ROWS, 16), 2 * ROWS)
            high_ref[here] = high
            low_ref[here] = low

        here = slice(n * group * ROWS, (n + 1) * group * ROWS)
        result = dot(high_ref[here], tz[...]) + dot(low_ref[here], tz[...])
        result = result[:, :128] + result[:, 128:]
        along_z[n * group : (n + 1) * group] = result.reshape(group, ROWS, 128)

    for copy in copies[6:]:
        copy.wait()
    lane = lax.broadcasted_iota(jnp.int32, (8, 128), 1)
    real_lane = rem(lane, 2 * KZ) < KZ
    turn_sign = jnp.where(real_lane, 1.0, -1.0)
    modes = [[], []]
    for a in range(ROWS // 8):
        here = slice(a * 8, a * 8 + 8)
        first, middle = along_z[0, here], along_z[CHUNKS // 2, here]
        even, odd = [], []
        for t in range(1, CHUNKS // 2):
            one, other = along_z[t, here], along_z[CHUNKS - t, here]
            even.append(one + other)
            odd.append(one - other)
        placed = [[None, None], [None, None]]
        for k in range(KY):
            total_cos = first + middle if k % 2 == 0 else first - middle
            total_sin = None
            for t in range(1, CHUNKS // 2):
                angle = 2 * math.pi * (k * t % CHUNKS) / CHUNKS
                total_cos = total_cos + even[t - 1] * math.cos(angle)
                term = odd[t - 1] * math.sin(angle)
                total_sin = term if total_sin is None else total_sin + term
            cosine, sine = ty[k : k + 1], ty[KY + k : KY + k + 1]
            same = cosine * total_cos - sine * total_sin
            cross = sine * total_cos + cosine * total_sin
            for shift in (2 * KZ, 4 * KZ):
                same = same + pltpu.roll(same, shift, 1)
                cross = cross + pltpu.roll(cross, shift, 1)
            cross = pltpu.roll(cross, KZ, 1) * turn_sign
            plus, minus = same + cross, same - cross
            real = jnp.where(real_lane, plus, pltpu.roll(minus, KZ, 1))
            imag = jnp.where(real_lane, pltpu.roll(plus, KZ, 1), minus)
            if k == 0:
                real, imag = jnp.where(real_lane, real, 0.0), jnp.where(real_lane, imag, 0.0)
            spot = lane // (2 * KZ) == k % 4
            for c, value in enumerate((real, imag)):
                old = placed[c][k // 4]
                placed[c][k // 4] = value if old is None else jnp.where(spot, value, old)
        for c in range(2):
            modes[c].append(jnp.concatenate(placed[c], 1))
    high, low = halves(jnp.concatenate(modes[0] + modes[1], 0))
    left[: 2 * ROWS] = high
    left[2 * ROWS : 4 * ROWS] = low
    left[4 * ROWS :] = tx[...]

    pl.semaphore_wait(barrier, greeted)
    upper = upper[:, :BLOCK]

    def to_group(n, slot, peer):
        return pltpu.make_async_remote_copy(
            part.at[n], landed.at[slot], send1.at[n], recv1.at[slot], device_id=(i, peer), device_id_type=MESH
        )

    sent = []
    for n, (e, d) in enumerate(OFFSETS):
        peer = ga_at(zl + turn * e, x + d)
        block = ga_at(zl + turn * e + 2, x + d + 4 - y)
        picked = dot(left[...], hot[block, :256])
        real = imag = jnp.zeros((8, BLOCK), jnp.float32)
        for a in range(ROWS // 8):
            re, im, cosine, sine = [
                picked[s * ROWS + a * 8 : s * ROWS + a * 8 + 8]
                + picked[s * ROWS + lag * ROWS + a * 8 : s * ROWS + lag * ROWS + a * 8 + 8]
                for s, lag in ((0, 2), (1, 2), (4, 2), (5, 2))
            ]
            real = real + cosine * re + sine * im
            imag = imag + cosine * im - sine * re
        imag = imag * hot[block, 256:].astype(jnp.float32)[:8]
        real = real + pltpu.roll(real, HERE, 0)
        imag = imag + pltpu.roll(imag, HERE, 0)
        part[n] = jnp.where(upper, real, imag) * scale
        if n < GROUPS - 1:
            copy = to_group(n, j, peer)
            copy.start()
            sent.append(copy)

    value = part[GROUPS - 1]
    for n, (e, d) in reversed(list(enumerate(OFFSETS[:-1]))):
        peer = ga_at(zl + turn * e, x + d)
        to_group(n, peer, peer).wait_recv()
        value = value + landed[peer]
    total[...] = value

    def col_slot(zh, y, core):
        return zh * 8 + y * 2 + core

    def row_slot(zh, y, core):
        return zh * 8 + core * 4 + y

    def col_copy(n, to_z, h, s):
        return pltpu.make_async_remote_copy(
            total, cols.at[s], send_col.at[n], recv_col.at[h], device_id=(mine, ga_at(to_z, x)), device_id_type=MESH
        )

    my_col = col_slot(zh, y, core)
    lift = jnp.where(mine // 8 == zh, 2, 0)

    @pl.when(own)
    def _():
        cols[my_col] = total[...]

    for n, d in enumerate((0, 1, 3, 2)):
        to_z = rem(zl + lift + d, 4)

        @pl.when(jnp.logical_not(jnp.logical_and(own, to_z == zl)))
        def _():
            col_copy(n, to_z, zh * 2 + core, my_col).start()

    def row_copy(n, to_h, to_y, h, s):
        return pltpu.make_async_remote_copy(
            total, rows.at[s], send_row.at[n], recv_row.at[h],
            device_id=(pair_at(to_h, to_y, core), mine), device_id_type=MESH,
        )

    my_row = row_slot(zh, y, core)
    targets = [(h, d) for d in (2, 1, 3, 0) for h in range(2)]
    for n, (h, d) in enumerate(targets):
        row_copy(n, h, y + d, y * 2 + zh, my_row).start()

    def pass_col(n, d, slot, sem):
        two = cols.at[pl.ds(slot, 2)]
        return pltpu.make_async_remote_copy(
            two, two, send_fc.at[n], recv_fc.at[sem], device_id=(i, ga_at(zl, x + d)), device_id_type=MESH
        )

    def pass_row(h, c):
        four = rows.at[pl.ds(row_slot(h, 0, c), 4)]
        return pltpu.make_async_remote_copy(
            four, four, send_fr.at[h], recv_fr.at[h], device_id=(sibling, j), device_id_type=MESH
        )

    def wait_rows(h):
        for d in (0, 1, 3, 2):
            from_y = rem(y + d, 4)
            row_copy(0, h, from_y, from_y * 2 + h, row_slot(h, from_y, core)).wait_recv()
        pass_row(h, core).start()

    def wait_cols(step, h):
        for c in range(2):
            self_sent = jnp.logical_and(own, jnp.logical_and(h == zh, core == c))

            @pl.when(jnp.logical_not(self_sent))
            def _():
                col_copy(0, zl, h * 2 + c, col_slot(h, col_y, c)).wait_recv()

        for n, d in enumerate((2, 1, 3)):
            pass_col(step * 3 + n, d, col_slot(h, col_y, 0), col_y * 2 + h).start()

    halfs = (zh, 1 - zh)
    for step, h in enumerate(halfs):
        wait_cols(step, h)
        wait_rows(h)

    for copy in sent:
        copy.wait_send()
    for n, d in enumerate((0, 1, 3, 2)):
        to_z = rem(zl + lift + d, 4)

        @pl.when(jnp.logical_not(jnp.logical_and(own, to_z == zl)))
        def _():
            col_copy(n, to_z, zh * 2 + core, my_col).wait_send()

    for n, (h, d) in enumerate(targets):
        row_copy(n, h, y + d, y * 2 + zh, my_row).wait_send()

    for step, h in enumerate(halfs):
        pass_row(h, core).wait_send()
        pass_row(h, 1 - core).wait_recv()
        high, low = halves(jnp.concatenate([rows[h * 8 + c * 4 + y] for y in range(4) for c in range(2)], 0).T)
        turned = jnp.concatenate([high, high, low], 1)
        for n, d in enumerate((2, 1, 3)):
            pass_col(step * 3 + n, d, col_slot(h, col_y, 0), col_y * 2 + h).wait_send()
        for n, d in enumerate((1, 3, 2)):
            from_y = rem(col_y + d, 4)
            pass_col(0, d, col_slot(h, from_y, 0), from_y * 2 + h).wait_recv()
        blocks = -cols[pl.ds(h * 8, 8)]
        swapped = jnp.concatenate([-blocks[:, HERE:], blocks[:, :HERE]], 1)
        for o, value in enumerate((blocks, swapped)):
            high, low = halves(value.reshape(PAIRS, BLOCK))
            value = dot(turned, jnp.concatenate([high, low, high], 0))
            out[o] = value if step == 0 else out[o] + value


def coefficients(owner, pairs, energy_v, energy_c, sphere, orbitals):
    vmem = pl.BlockSpec(memory_space=pltpu.VMEM)
    hbm = pl.BlockSpec(memory_space=pl.ANY)
    points = NY * NZ
    dma = pltpu.SemaphoreType.DMA
    return pl.pallas_call(
        coefficients_kernel,
        out_shape=jax.ShapeDtypeStruct((2, BLOCK, BLOCK), jnp.float32),
        in_specs=[hbm] * 9,
        out_specs=vmem,
        scratch_shapes=[
            pltpu.SMEM((2, 8), jnp.int32),
            pltpu.SMEM((2, HERE), jnp.int32),
            pltpu.SMEM((8,), jnp.float32),
            pltpu.SMEM((8,), jnp.float32),
            pltpu.VMEM((1, NG), jnp.int32),
            pltpu.VMEM((16 * PLANES, points), jnp.bfloat16),
            pltpu.VMEM((WIDE, 256), jnp.bfloat16),
            pltpu.VMEM((2 * KY, 128), jnp.float32),
            pltpu.VMEM((4 * ROWS, 256), jnp.bfloat16),
            pltpu.VMEM((CHUNKS * ROWS, WIDE), jnp.bfloat16),
            pltpu.VMEM((CHUNKS * ROWS, WIDE), jnp.bfloat16),
            pltpu.VMEM((CHUNKS, ROWS, 128), jnp.float32),
            pltpu.VMEM((GROUPS, 256 + 16, BLOCK), jnp.bfloat16),
            pltpu.VMEM((8 * ROWS, 256), jnp.bfloat16),
            pltpu.VMEM((GROUPS, 8, BLOCK), jnp.float32),
            pltpu.VMEM((GROUPS, 8, BLOCK), jnp.float32),
            pltpu.VMEM((8, BLOCK), jnp.float32),
            pltpu.VMEM((GROUPS, 8, BLOCK), jnp.float32),
            pltpu.VMEM((GROUPS, 8, BLOCK), jnp.float32),
            dma((LOADS + 8,)), dma((GROUPS,)), dma((GROUPS,)), dma((4,)), dma((4,)), dma((8,)), dma((8,)),
            dma((6,)), dma((8,)), dma((2,)), dma((2,)),
        ],
        compiler_params=pltpu.CompilerParams(
            collective_id=0, has_side_effects=True, vmem_limit_bytes=40 * 1024 * 1024
        ),
        name="coefficients",
    )(*[
        pltpu.with_memory_space_constraint(value, pltpu.HBM)
        for value in (
            owner, pairs.T, energy_v, energy_c, sphere.reshape(1, NG),
            orbitals.transpose(0, 2, 1, 3).reshape(16 * PLANES, points),
            jnp.asarray(table_along_z()), jnp.asarray(twiddles()), jnp.asarray(table_along_x()),
        )
    ])


def per_device(orbitals, owner, pair_list, valence_energy, conduction_energy, sphere_index):
    return coefficients(owner, pair_list, valence_energy, conduction_energy, sphere_index, orbitals)


def solution(mesh):
    return jax.shard_map(
        per_device,
        mesh=mesh,
        in_specs=(P(None, None, "ga", None), P(), P("pair", None), P(), P(), P()),
        out_specs=P(None, "ga", "pair"),
        check_vma=False,
    )
```

```python
import math

import jax
import jax.numpy as jnp
import ml_dtypes
import numpy as np
from jax import lax
from jax.experimental import pallas as pl
from jax.experimental.pallas import tpu as pltpu
from jax.sharding import PartitionSpec as P

NX = 96
NY = 96
NZ = 192
NG = 4096
PAIRS = 64
GROUPS = 16
PLANES = NX // GROUPS
HERE = PAIRS // GROUPS
ROWS = PLANES * HERE
STEP = 4
CHUNKS = NY // STEP
WIDE = STEP * NZ
KY = 8
KZ = 16
KX = 7
BLOCK = NG // GROUPS
LOADS = 4
MESH = pl.DeviceIdType.MESH
OFFSETS = sorted(((e, d) for e in range(4) for d in range(4)), key=lambda o: -(o[0] + min(o[1], 4 - o[1])))


def split(table):
    high = table.astype(ml_dtypes.bfloat16)
    low = (table - high.astype(np.float64)).astype(ml_dtypes.bfloat16)
    return high, low


def table_along_z():
    angle = 2 * math.pi * (np.arange(NZ)[:, None] * np.arange(KZ)[None, :] % NZ) / NZ
    table = np.zeros((STEP, NZ, STEP, 2, KZ))
    for r in range(STEP):
        table[r, :, r, 0] = np.cos(angle)
        table[r, :, r, 1] = -np.sin(angle)
    return np.concatenate(split(table.reshape(WIDE, STEP * 2 * KZ)), 1)


def twiddles():
    angle = 2 * math.pi * np.arange(KY)[:, None] * np.arange(STEP)[None, :] / NY
    angle = np.repeat(angle, 2 * KZ, 1)
    return np.concatenate([np.cos(angle), np.sin(angle)]).astype(np.float32)


def table_along_x():
    table = np.zeros((GROUPS, 2, PLANES, HERE, 256))
    for j in range(GROUPS):
        for x in range(PLANES):
            for f in range(-KX, KX + 1):
                angle = 2 * math.pi * (f * (PLANES * j + x) % NX) / NX
                table[j, 0, x, :, 16 + f + KX] = math.cos(angle)
                table[j, 1, x, :, 16 + f + KX] = math.sin(angle)
    high, low = split(table.reshape(GROUPS, 2 * ROWS, 256))
    return np.concatenate([high, low], 1)


def halves(value):
    high = value.astype(jnp.bfloat16)
    return high, (value - high.astype(jnp.float32)).astype(jnp.bfloat16)


def dot(left, right):
    return jnp.dot(left, right, preferred_element_type=jnp.float32)


def rem(value, size):
    return lax.rem(value, size)


def coefficients_kernel(
    owner_in, pairs_in, energy_v_in, energy_c_in, sphere_in, orbitals, table_z, table_y, table_x, out,
    owner, pairs, energy_v, energy_c, sphere, orb, tz, ty, tx, high_ref, low_ref, along_z, hot, left, part, landed, total,
    rows, cols, sems, send1, recv1, send_col, recv_col, send_row, recv_row, send_fc, recv_fc, send_fr, recv_fr,
):
    i, j = lax.axis_index("pair"), lax.axis_index("ga")
    zh, y, core = i // 8, rem(i // 2, 4), rem(i, 2)
    zl, x = j // 4, rem(j, 4)
    sibling = i + 1 - 2 * core

    def pair_at(zh, y, core):
        return zh * 8 + rem(y, 4) * 2 + core

    def ga_at(zl, x):
        return rem(zl, 4) * 4 + rem(x, 4)

    def mix(a, b):
        return rem(a // 2 + b // 2, 2) * 2 + rem(a + b, 2)

    def block_at(zl, x):
        return mix(rem(zl + 2, 4), rem(y, 2)) * 4 + mix(x, y)

    mine = block_at(zl, x)
    own = mine == i
    col_y = mix(x, rem(i, 4))

    moves = (
        (owner_in, owner), (pairs_in, pairs), (energy_v_in, energy_v), (energy_c_in, energy_c), (sphere_in, sphere),
        (table_z, tz), (table_x.at[j], tx), (table_y, ty),
    )
    copies = [pltpu.make_async_copy(source, target, sems.at[LOADS + n]) for n, (source, target) in enumerate(moves)]
    loads = []
    span = CHUNKS // LOADS * WIDE
    for n in range(LOADS):
        lanes = pl.ds(n * span, span)
        loads.append(pltpu.make_async_copy(orbitals.at[:, lanes], orb.at[:, lanes], sems.at[n]))
    for copy in copies[4:5] + loads[:1] + copies[:4] + copies[5:6] + loads[1:] + copies[6:]:
        copy.start()

    barrier = pltpu.get_barrier_semaphore()

    def greet(device):
        pl.semaphore_signal(barrier, inc=1, device_id=device, device_id_type=MESH)

    turn = jnp.where(zl < 2, 1, 3)
    for e, d in OFFSETS[:-1]:
        greet((i, ga_at(zl + turn * e, x + d)))
    across = ga_at(jnp.where(zl < 2, 3, 0), x)
    for d in (2, 1, 3, 0):
        greet((pair_at(1 - zh, y + d, core), across))
    greet((pair_at(1 - zh, col_y, 1 - core), across))
    for d in (2, 1, 3):
        greet((pair_at(zh, y + d, core), j))
    greet((pair_at(zh, col_y, 1 - core), j))
    greet((sibling, j))
    side = jnp.where(rem(zl, 3) == 0, 1, 0)
    even = rem(x + y + core, 2)
    greeted = (GROUPS - 1) + 4 + 8 * side + even * (2 + 4 * side)

    copies[4].wait()
    position = sphere[...]
    column = lax.shift_right_logical(lax.shift_right_logical(position, 6) * 43691, 17)
    index_z = position - column * NZ
    index_x = lax.shift_right_logical(lax.shift_right_logical(column, 5) * 43691, 17)
    index_y = column - index_x * NY
    freq_x = jnp.where(index_x >= NX // 2, index_x - NX, index_x)
    freq_y = jnp.where(index_y >= NY // 2, index_y - NY, index_y)
    freq_z = jnp.where(index_z >= NZ // 2, index_z - NZ, index_z)
    flip = freq_z < 0
    freq_x = jnp.where(flip, -freq_x, freq_x) + KX
    freq_y = jnp.where(flip, -freq_y, freq_y)
    mode = jnp.abs(freq_y) * 32 + jnp.where(freq_y < 0, 16, 0) + jnp.abs(freq_z)
    sign = jnp.where(flip, -1.0, 1.0)
    row = lax.broadcasted_iota(jnp.int32, (256, BLOCK), 0)
    for b in range(GROUPS):
        lanes = slice(b * BLOCK, (b + 1) * BLOCK)
        hot[b, :256] = jnp.where(row == mode[:, lanes], 1.0, 0.0).astype(jnp.bfloat16)
        hot[b, 16:32] = jnp.where(row[:16] == freq_x[:, lanes], 1.0, 0.0).astype(jnp.bfloat16)
        hot[b, 256:] = jnp.broadcast_to(sign[:, lanes], (16, BLOCK)).astype(jnp.bfloat16)

    for copy in copies[:4]:
        copy.wait()
    place = rem(lax.broadcasted_iota(jnp.int32, (8, WIDE), 0), HERE)
    slot_v = jnp.zeros((8, WIDE), jnp.int32)
    slot_c = jnp.zeros((8, WIDE), jnp.int32)
    gap = jnp.zeros((8, BLOCK), jnp.float32)
    for p in range(HERE):
        v, c = pairs[0, p], pairs[1, p]
        slot_v = jnp.where(place == p, owner[0, v], slot_v)
        slot_c = jnp.where(place == p, owner[1, c], slot_c)
        gap = jnp.where(place[:, :BLOCK] == p, energy_c[c] - energy_v[v], gap)
    scale = jnp.sqrt(2.0 / gap) * (1.0 / math.sqrt(NX * NY * NZ * math.sqrt(PAIRS)))

    upper = lax.broadcasted_iota(jnp.int32, (8, WIDE), 0) < HERE

    def pick(value, slots):
        return jnp.take_along_axis(value, slots, axis=0, mode="promise_in_bounds")

    copies[5].wait()
    group = CHUNKS // LOADS

    def multiply(u):
        values = []
        for s in range(2):
            lanes = pl.ds(pl.multiple_of((2 * u + s) * WIDE, 128), WIDE)
            for a in range(PLANES // 2):
                val = orb[16 * a : 16 * a + 16, lanes].astype(jnp.float32)
                con = orb[48 + 16 * a : 64 + 16 * a, lanes].astype(jnp.float32)
                first = pick(val[:8], slot_v) * pick(con[:8], slot_c)
                second = pick(val[8:], slot_v) * pick(con[8:], slot_c)
                values.append(jnp.where(upper, first, second))
        high, low = halves(jnp.concatenate(values, 0))
        here = pl.ds(pl.multiple_of(u * 2 * ROWS, 16), 2 * ROWS)
        high_ref[here] = high
        low_ref[here] = low

    def transform(n):
        here = slice(n * group * ROWS, (n + 1) * group * ROWS)
        result = dot(high_ref[here], tz[...]) + dot(low_ref[here], tz[...])
        result = result[:, :128] + result[:, 128:]
        along_z[n * group : (n + 1) * group] = result.reshape(group, ROWS, 128)

    for n in range(LOADS):
        loads[n].wait()
        if n > 0:
            transform(n - 1)
        for u in range(n * group // 2, (n + 1) * group // 2):
            multiply(u)
    transform(LOADS - 1)

    for copy in copies[6:]:
        copy.wait()
    lane = lax.broadcasted_iota(jnp.int32, (8, 128), 1)
    real_lane = rem(lane, 2 * KZ) < KZ
    turn_sign = jnp.where(real_lane, 1.0, -1.0)
    modes = [[], []]
    for a in range(ROWS // 8):
        here = slice(a * 8, a * 8 + 8)
        first, middle = along_z[0, here], along_z[CHUNKS // 2, here]
        even, odd = [], []
        for t in range(1, CHUNKS // 2):
            one, other = along_z[t, here], along_z[CHUNKS - t, here]
            even.append(one + other)
            odd.append(one - other)
        placed = [[None, None], [None, None]]
        for k in range(KY):
            total_cos = first + middle if k % 2 == 0 else first - middle
            total_sin = None
            for t in range(1, CHUNKS // 2):
                angle = 2 * math.pi * (k * t % CHUNKS) / CHUNKS
                total_cos = total_cos + even[t - 1] * math.cos(angle)
                term = odd[t - 1] * math.sin(angle)
                total_sin = term if total_sin is None else total_sin + term
            cosine, sine = ty[k : k + 1], ty[KY + k : KY + k + 1]
            same = cosine * total_cos - sine * total_sin
            cross = sine * total_cos + cosine * total_sin
            for shift in (2 * KZ, 4 * KZ):
                same = same + pltpu.roll(same, shift, 1)
                cross = cross + pltpu.roll(cross, shift, 1)
            cross = pltpu.roll(cross, KZ, 1) * turn_sign
            plus, minus = same + cross, same - cross
            real = jnp.where(real_lane, plus, pltpu.roll(minus, KZ, 1))
            imag = jnp.where(real_lane, pltpu.roll(plus, KZ, 1), minus)
            if k == 0:
                real, imag = jnp.where(real_lane, real, 0.0), jnp.where(real_lane, imag, 0.0)
            spot = lane // (2 * KZ) == k % 4
            for c, value in enumerate((real, imag)):
                old = placed[c][k // 4]
                placed[c][k // 4] = value if old is None else jnp.where(spot, value, old)
        for c in range(2):
            modes[c].append(jnp.concatenate(placed[c], 1))
    high, low = halves(jnp.concatenate(modes[0] + modes[1], 0))
    left[: 2 * ROWS] = high
    left[2 * ROWS : 4 * ROWS] = low
    left[4 * ROWS :] = tx[...]

    pl.semaphore_wait(barrier, greeted)
    upper = upper[:, :BLOCK]

    def to_group(n, slot, peer):
        return pltpu.make_async_remote_copy(
            part.at[n], landed.at[slot], send1.at[n], recv1.at[slot], device_id=(i, peer), device_id_type=MESH
        )

    sent = []
    for n, (e, d) in enumerate(OFFSETS):
        peer = ga_at(zl + turn * e, x + d)
        block = block_at(rem(zl + turn * e, 4), rem(x + d, 4))
        picked = dot(left[...], hot[block, :256])
        real = imag = jnp.zeros((8, BLOCK), jnp.float32)
        for a in range(ROWS // 8):
            re, im, cosine, sine = [
                picked[s * ROWS + a * 8 : s * ROWS + a * 8 + 8]
                + picked[s * ROWS + lag * ROWS + a * 8 : s * ROWS + lag * ROWS + a * 8 + 8]
                for s, lag in ((0, 2), (1, 2), (4, 2), (5, 2))
            ]
            real = real + cosine * re + sine * im
            imag = imag + cosine * im - sine * re
        imag = imag * hot[block, 256:].astype(jnp.float32)[:8]
        real = real + pltpu.roll(real, HERE, 0)
        imag = imag + pltpu.roll(imag, HERE, 0)
        part[n] = jnp.where(upper, real, imag) * scale
        if n < GROUPS - 1:
            copy = to_group(n, j, peer)
            copy.start()
            sent.append(copy)

    value = part[GROUPS - 1]
    for n, (e, d) in reversed(list(enumerate(OFFSETS[:-1]))):
        peer = ga_at(zl + turn * e, x + d)
        to_group(n, peer, peer).wait_recv()
        value = value + landed[peer]
    total[...] = value

    def col_slot(zh, y, core):
        return zh * 8 + y * 2 + core

    def row_slot(zh, y, core):
        return zh * 8 + core * 4 + y

    def col_copy(n, to_z, h, s):
        return pltpu.make_async_remote_copy(
            total, cols.at[s], send_col.at[n], recv_col.at[h], device_id=(mine, ga_at(to_z, x)), device_id_type=MESH
        )

    my_col = col_slot(zh, y, core)
    lift = jnp.where(mine // 8 == zh, 2, 0)

    @pl.when(own)
    def _():
        cols[my_col] = total[...]

    for n, d in enumerate((0, 1, 3, 2)):
        to_z = rem(zl + lift + d, 4)

        @pl.when(jnp.logical_not(jnp.logical_and(own, to_z == zl)))
        def _():
            col_copy(n, to_z, zh * 2 + core, my_col).start()

    def row_copy(n, to_h, to_y, h, s):
        return pltpu.make_async_remote_copy(
            total, rows.at[s], send_row.at[n], recv_row.at[h],
            device_id=(pair_at(to_h, to_y, core), mine), device_id_type=MESH,
        )

    my_row = row_slot(zh, y, core)
    targets = [(h, d) for d in (2, 1, 3, 0) for h in range(2)]
    for n, (h, d) in enumerate(targets):
        row_copy(n, h, y + d, y * 2 + zh, my_row).start()

    def pass_col(n, d, slot, sem):
        two = cols.at[pl.ds(slot, 2)]
        return pltpu.make_async_remote_copy(
            two, two, send_fc.at[n], recv_fc.at[sem], device_id=(i, ga_at(zl, x + d)), device_id_type=MESH
        )

    def pass_row(h, c):
        four = rows.at[pl.ds(row_slot(h, 0, c), 4)]
        return pltpu.make_async_remote_copy(
            four, four, send_fr.at[h], recv_fr.at[h], device_id=(sibling, j), device_id_type=MESH
        )

    def wait_rows(h):
        for d in (0, 1, 3, 2):
            from_y = rem(y + d, 4)
            row_copy(0, h, from_y, from_y * 2 + h, row_slot(h, from_y, core)).wait_recv()
        pass_row(h, core).start()

    def wait_cols(step, h):
        for c in range(2):
            self_sent = jnp.logical_and(own, jnp.logical_and(h == zh, core == c))

            @pl.when(jnp.logical_not(self_sent))
            def _():
                col_copy(0, zl, h * 2 + c, col_slot(h, col_y, c)).wait_recv()

        for n, d in enumerate((2, 1, 3)):
            pass_col(step * 3 + n, d, col_slot(h, col_y, 0), col_y * 2 + h).start()

    halfs = (zh, 1 - zh)
    for step, h in enumerate(halfs):
        wait_cols(step, h)
        wait_rows(h)

    for copy in sent:
        copy.wait_send()
    for n, d in enumerate((0, 1, 3, 2)):
        to_z = rem(zl + lift + d, 4)

        @pl.when(jnp.logical_not(jnp.logical_and(own, to_z == zl)))
        def _():
            col_copy(n, to_z, zh * 2 + core, my_col).wait_send()

    for n, (h, d) in enumerate(targets):
        row_copy(n, h, y + d, y * 2 + zh, my_row).wait_send()

    for step, h in enumerate(halfs):
        pass_row(h, core).wait_send()
        pass_row(h, 1 - core).wait_recv()
        high, low = halves(jnp.concatenate([rows[h * 8 + c * 4 + y] for y in range(4) for c in range(2)], 0).T)
        turned = jnp.concatenate([high, high, low], 1)
        for n, d in enumerate((2, 1, 3)):
            pass_col(step * 3 + n, d, col_slot(h, col_y, 0), col_y * 2 + h).wait_send()
        for n, d in enumerate((1, 3, 2)):
            from_y = mix(rem(x + d, 4), rem(i, 4))
            pass_col(0, d, col_slot(h, from_y, 0), from_y * 2 + h).wait_recv()
        blocks = -cols[pl.ds(h * 8, 8)]
        swapped = jnp.concatenate([-blocks[:, HERE:], blocks[:, :HERE]], 1)
        for o, value in enumerate((blocks, swapped)):
            high, low = halves(value.reshape(PAIRS, BLOCK))
            value = dot(turned, jnp.concatenate([high, low, high], 0))
            out[o] = value if step == 0 else out[o] + value


def coefficients(owner, pairs, energy_v, energy_c, sphere, orbitals):
    vmem = pl.BlockSpec(memory_space=pltpu.VMEM)
    hbm = pl.BlockSpec(memory_space=pl.ANY)
    points = NY * NZ
    dma = pltpu.SemaphoreType.DMA
    return pl.pallas_call(
        coefficients_kernel,
        out_shape=jax.ShapeDtypeStruct((2, BLOCK, BLOCK), jnp.float32),
        in_specs=[hbm] * 9,
        out_specs=vmem,
        scratch_shapes=[
            pltpu.SMEM((2, 8), jnp.int32),
            pltpu.SMEM((2, HERE), jnp.int32),
            pltpu.SMEM((8,), jnp.float32),
            pltpu.SMEM((8,), jnp.float32),
            pltpu.VMEM((1, NG), jnp.int32),
            pltpu.VMEM((16 * PLANES, points), jnp.bfloat16),
            pltpu.VMEM((WIDE, 256), jnp.bfloat16),
            pltpu.VMEM((2 * KY, 128), jnp.float32),
            pltpu.VMEM((4 * ROWS, 256), jnp.bfloat16),
            pltpu.VMEM((CHUNKS * ROWS, WIDE), jnp.bfloat16),
            pltpu.VMEM((CHUNKS * ROWS, WIDE), jnp.bfloat16),
            pltpu.VMEM((CHUNKS, ROWS, 128), jnp.float32),
            pltpu.VMEM((GROUPS, 256 + 16, BLOCK), jnp.bfloat16),
            pltpu.VMEM((8 * ROWS, 256), jnp.bfloat16),
            pltpu.VMEM((GROUPS, 8, BLOCK), jnp.float32),
            pltpu.VMEM((GROUPS, 8, BLOCK), jnp.float32),
            pltpu.VMEM((8, BLOCK), jnp.float32),
            pltpu.VMEM((GROUPS, 8, BLOCK), jnp.float32),
            pltpu.VMEM((GROUPS, 8, BLOCK), jnp.float32),
            dma((LOADS + 8,)), dma((GROUPS,)), dma((GROUPS,)), dma((4,)), dma((4,)), dma((8,)), dma((8,)),
            dma((6,)), dma((8,)), dma((2,)), dma((2,)),
        ],
        compiler_params=pltpu.CompilerParams(
            collective_id=0, has_side_effects=True, vmem_limit_bytes=40 * 1024 * 1024
        ),
        name="coefficients",
    )(*[
        pltpu.with_memory_space_constraint(value, pltpu.HBM)
        for value in (
            owner, pairs.T, energy_v, energy_c, sphere.reshape(1, NG),
            orbitals.transpose(0, 2, 1, 3).reshape(16 * PLANES, points),
            jnp.asarray(table_along_z()), jnp.asarray(twiddles()), jnp.asarray(table_along_x()),
        )
    ])


def per_device(orbitals, owner, pair_list, valence_energy, conduction_energy, sphere_index):
    return coefficients(owner, pair_list, valence_energy, conduction_energy, sphere_index, orbitals)


def solution(mesh):
    return jax.shard_map(
        per_device,
        mesh=mesh,
        in_specs=(P(None, None, "ga", None), P(), P("pair", None), P(), P(), P()),
        out_specs=P(None, "ga", "pair"),
        check_vma=False,
    )
```

```python
import math

import jax
import jax.numpy as jnp
import ml_dtypes
import numpy as np
from jax import lax
from jax.experimental import pallas as pl
from jax.experimental.pallas import tpu as pltpu
from jax.sharding import PartitionSpec as P

NX = 96
NY = 96
NZ = 192
NG = 4096
PAIRS = 64
GROUPS = 16
PLANES = NX // GROUPS
HERE = PAIRS // GROUPS
ROWS = PLANES * HERE
STEP = 4
CHUNKS = NY // STEP
WIDE = STEP * NZ
KY = 8
KZ = 16
KX = 7
BLOCK = NG // GROUPS
LOADS = 4
MESH = pl.DeviceIdType.MESH
OFFSETS = sorted(((e, d) for e in range(4) for d in range(4)), key=lambda o: -(o[0] + min(o[1], 4 - o[1])))


def split(table):
    high = table.astype(ml_dtypes.bfloat16)
    low = (table - high.astype(np.float64)).astype(ml_dtypes.bfloat16)
    return high, low


def table_along_z():
    angle = 2 * math.pi * (np.arange(NZ)[:, None] * np.arange(KZ)[None, :] % NZ) / NZ
    table = np.zeros((STEP, NZ, STEP, 2, KZ))
    for r in range(STEP):
        table[r, :, r, 0] = np.cos(angle)
        table[r, :, r, 1] = -np.sin(angle)
    return np.concatenate(split(table.reshape(WIDE, STEP * 2 * KZ)), 1)


def twiddles():
    angle = 2 * math.pi * np.arange(KY)[:, None] * np.arange(STEP)[None, :] / NY
    angle = np.repeat(angle, 2 * KZ, 1)
    return np.concatenate([np.cos(angle), np.sin(angle)]).astype(np.float32)


def table_along_x():
    table = np.zeros((GROUPS, 2, PLANES, HERE, 256))
    for j in range(GROUPS):
        for x in range(PLANES):
            for f in range(-KX, KX + 1):
                angle = 2 * math.pi * (f * (PLANES * j + x) % NX) / NX
                table[j, 0, x, :, 16 + f + KX] = math.cos(angle)
                table[j, 1, x, :, 16 + f + KX] = math.sin(angle)
    high, low = split(table.reshape(GROUPS, 2 * ROWS, 256))
    return np.concatenate([high, low], 1)


def halves(value):
    high = value.astype(jnp.bfloat16)
    return high, (value - high.astype(jnp.float32)).astype(jnp.bfloat16)


def dot(left, right):
    return jnp.dot(left, right, preferred_element_type=jnp.float32)


def rem(value, size):
    return lax.rem(value, size)


def coefficients_kernel(
    owner_in, pairs_in, energy_v_in, energy_c_in, sphere_in, orbitals, table_z, table_y, table_x, out,
    owner, pairs, energy_v, energy_c, sphere, orb, tz, ty, tx, split_ref, along_z, hot, left, part, landed, total,
    rows, cols, sems, send1, recv1, send_col, recv_col, send_row, recv_row, send_fc, recv_fc, send_fr, recv_fr,
):
    i, j = lax.axis_index("pair"), lax.axis_index("ga")
    zh, y, core = i // 8, rem(i // 2, 4), rem(i, 2)
    zl, x = j // 4, rem(j, 4)
    sibling = i + 1 - 2 * core

    def pair_at(zh, y, core):
        return zh * 8 + rem(y, 4) * 2 + core

    def ga_at(zl, x):
        return rem(zl, 4) * 4 + rem(x, 4)

    mine = ga_at(zl + 2, x + 4 - y)
    own = mine == i
    col_y = rem(x + 4 - rem(i, 4), 4)

    moves = (
        (owner_in, owner), (pairs_in, pairs), (energy_v_in, energy_v), (energy_c_in, energy_c), (sphere_in, sphere),
        (table_z, tz), (table_x.at[j], tx), (table_y, ty),
    )
    copies = [pltpu.make_async_copy(source, target, sems.at[LOADS + n]) for n, (source, target) in enumerate(moves)]
    loads = []
    span = CHUNKS // LOADS * WIDE
    for n in range(LOADS):
        lanes = pl.ds(n * span, span)
        loads.append(pltpu.make_async_copy(orbitals.at[:, lanes], orb.at[:, lanes], sems.at[n]))
    for copy in copies[4:5] + loads[:1] + copies[:4] + copies[5:6] + loads[1:] + copies[6:]:
        copy.start()

    barrier = pltpu.get_barrier_semaphore()

    def greet(device):
        pl.semaphore_signal(barrier, inc=1, device_id=device, device_id_type=MESH)

    turn = jnp.where(zl < 2, 1, 3)
    for e, d in OFFSETS[:-1]:
        greet((i, ga_at(zl + turn * e, x + d)))
    across = ga_at(jnp.where(zl < 2, 3, 0), x)
    for d in (2, 1, 3, 0):
        greet((pair_at(1 - zh, y + d, core), across))
    greet((pair_at(1 - zh, col_y, 1 - core), across))
    for d in (2, 1, 3):
        greet((pair_at(zh, y + d, core), j))
    greet((pair_at(zh, col_y, 1 - core), j))
    greet((sibling, j))
    side = jnp.where(rem(zl, 3) == 0, 1, 0)
    even = 1 - rem(x + 4 - (1 - core) + y, 2)
    greeted = (GROUPS - 1) + 4 + 8 * side + even * (2 + 4 * side)

    copies[4].wait()
    position = sphere[...]
    column = lax.shift_right_logical(lax.shift_right_logical(position, 6) * 43691, 17)
    index_z = position - column * NZ
    index_x = lax.shift_right_logical(lax.shift_right_logical(column, 5) * 43691, 17)
    index_y = column - index_x * NY
    freq_x = jnp.where(index_x >= NX // 2, index_x - NX, index_x)
    freq_y = jnp.where(index_y >= NY // 2, index_y - NY, index_y)
    freq_z = jnp.where(index_z >= NZ // 2, index_z - NZ, index_z)
    flip = freq_z < 0
    freq_x = jnp.where(flip, -freq_x, freq_x) + KX
    freq_y = jnp.where(flip, -freq_y, freq_y)
    mode = jnp.abs(freq_y) * 32 + jnp.where(freq_y < 0, 16, 0) + jnp.abs(freq_z)
    sign = jnp.where(flip, -1.0, 1.0)
    row = lax.broadcasted_iota(jnp.int32, (256, BLOCK), 0)
    for b in range(GROUPS):
        lanes = slice(b * BLOCK, (b + 1) * BLOCK)
        hot[b, :256] = jnp.where(row == mode[:, lanes], 1.0, 0.0).astype(jnp.bfloat16)
        hot[b, 16:32] = jnp.where(row[:16] == freq_x[:, lanes], 1.0, 0.0).astype(jnp.bfloat16)
        hot[b, 256:] = jnp.broadcast_to(sign[:, lanes], (16, BLOCK)).astype(jnp.bfloat16)

    for copy in copies[:4]:
        copy.wait()
    place = rem(lax.broadcasted_iota(jnp.int32, (8, WIDE), 0), HERE)
    slot_v = jnp.zeros((8, WIDE), jnp.int32)
    slot_c = jnp.zeros((8, WIDE), jnp.int32)
    gap = jnp.zeros((8, BLOCK), jnp.float32)
    for p in range(HERE):
        v, c = pairs[0, p], pairs[1, p]
        slot_v = jnp.where(place == p, owner[0, v], slot_v)
        slot_c = jnp.where(place == p, owner[1, c], slot_c)
        gap = jnp.where(place[:, :BLOCK] == p, energy_c[c] - energy_v[v], gap)
    scale = jnp.sqrt(2.0 / gap) * (1.0 / math.sqrt(NX * NY * NZ * math.sqrt(PAIRS)))

    upper = lax.broadcasted_iota(jnp.int32, (8, WIDE), 0) < HERE

    def pick(value, slots):
        return jnp.take_along_axis(value, slots, axis=0, mode="promise_in_bounds")

    copies[5].wait()
    group = CHUNKS // LOADS
    for n in range(LOADS):
        loads[n].wait()

        @pl.loop(n * group // 2, (n + 1) * group // 2, unroll=True)
        def _(u):
            values = []
            for s in range(2):
                lanes = pl.ds(pl.multiple_of((2 * u + s) * WIDE, 128), WIDE)
                for a in range(PLANES // 2):
                    val = orb[16 * a : 16 * a + 16, lanes].astype(jnp.float32)
                    con = orb[48 + 16 * a : 64 + 16 * a, lanes].astype(jnp.float32)
                    first = pick(val[:8], slot_v) * pick(con[:8], slot_c)
                    second = pick(val[8:], slot_v) * pick(con[8:], slot_c)
                    values.append(jnp.where(upper, first, second))
            high, low = halves(jnp.concatenate(values, 0))
            split_ref[n, pl.ds(pl.multiple_of((u - n * group // 2) * 2 * ROWS, 16), 2 * ROWS)] = high
            split_ref[n, pl.ds(pl.multiple_of((u - n * group // 2) * 2 * ROWS + group * ROWS, 16), 2 * ROWS)] = low

        result = dot(split_ref[n], tz[...])
        result = result[:, :128] + result[:, 128:]
        result = result[: group * ROWS] + result[group * ROWS :]
        along_z[n * group : (n + 1) * group] = result.reshape(group, ROWS, 128)

    for copy in copies[6:]:
        copy.wait()
    lane = lax.broadcasted_iota(jnp.int32, (8, 128), 1)
    real_lane = rem(lane, 2 * KZ) < KZ
    turn_sign = jnp.where(real_lane, 1.0, -1.0)
    modes = [[], []]
    for a in range(ROWS // 8):
        here = slice(a * 8, a * 8 + 8)
        first, middle = along_z[0, here], along_z[CHUNKS // 2, here]
        even, odd = [], []
        for t in range(1, CHUNKS // 2):
            one, other = along_z[t, here], along_z[CHUNKS - t, here]
            even.append(one + other)
            odd.append(one - other)
        placed = [[None, None], [None, None]]
        for k in range(KY):
            total_cos = first + middle if k % 2 == 0 else first - middle
            total_sin = None
            for t in range(1, CHUNKS // 2):
                angle = 2 * math.pi * (k * t % CHUNKS) / CHUNKS
                total_cos = total_cos + even[t - 1] * math.cos(angle)
                term = odd[t - 1] * math.sin(angle)
                total_sin = term if total_sin is None else total_sin + term
            cosine, sine = ty[k : k + 1], ty[KY + k : KY + k + 1]
            same = cosine * total_cos - sine * total_sin
            cross = sine * total_cos + cosine * total_sin
            for shift in (2 * KZ, 4 * KZ):
                same = same + pltpu.roll(same, shift, 1)
                cross = cross + pltpu.roll(cross, shift, 1)
            cross = pltpu.roll(cross, KZ, 1) * turn_sign
            plus, minus = same + cross, same - cross
            real = jnp.where(real_lane, plus, pltpu.roll(minus, KZ, 1))
            imag = jnp.where(real_lane, pltpu.roll(plus, KZ, 1), minus)
            if k == 0:
                real, imag = jnp.where(real_lane, real, 0.0), jnp.where(real_lane, imag, 0.0)
            spot = lane // (2 * KZ) == k % 4
            for c, value in enumerate((real, imag)):
                old = placed[c][k // 4]
                placed[c][k // 4] = value if old is None else jnp.where(spot, value, old)
        for c in range(2):
            modes[c].append(jnp.concatenate(placed[c], 1))
    high, low = halves(jnp.concatenate(modes[0] + modes[1], 0))
    left[: 2 * ROWS] = high
    left[2 * ROWS : 4 * ROWS] = low
    left[4 * ROWS :] = tx[...]

    pl.semaphore_wait(barrier, greeted)
    upper = upper[:, :BLOCK]

    def to_group(n, slot, peer):
        return pltpu.make_async_remote_copy(
            part.at[n], landed.at[slot], send1.at[n], recv1.at[slot], device_id=(i, peer), device_id_type=MESH
        )

    sent = []
    for n, (e, d) in enumerate(OFFSETS):
        peer = ga_at(zl + turn * e, x + d)
        block = ga_at(zl + turn * e + 2, x + d + 4 - y)
        picked = dot(left[...], hot[block, :256])
        real = imag = jnp.zeros((8, BLOCK), jnp.float32)
        for a in range(ROWS // 8):
            re, im, cosine, sine = [
                picked[s * ROWS + a * 8 : s * ROWS + a * 8 + 8]
                + picked[s * ROWS + lag * ROWS + a * 8 : s * ROWS + lag * ROWS + a * 8 + 8]
                for s, lag in ((0, 2), (1, 2), (4, 2), (5, 2))
            ]
            real = real + cosine * re + sine * im
            imag = imag + cosine * im - sine * re
        imag = imag * hot[block, 256:].astype(jnp.float32)[:8]
        real = real + pltpu.roll(real, HERE, 0)
        imag = imag + pltpu.roll(imag, HERE, 0)
        part[n] = jnp.where(upper, real, imag) * scale
        if n < GROUPS - 1:
            copy = to_group(n, j, peer)
            copy.start()
            sent.append(copy)

    value = part[GROUPS - 1]
    for n, (e, d) in reversed(list(enumerate(OFFSETS[:-1]))):
        peer = ga_at(zl + turn * e, x + d)
        to_group(n, peer, peer).wait_recv()
        value = value + landed[peer]
    total[...] = value

    def col_slot(zh, y, core):
        return zh * 8 + y * 2 + core

    def row_slot(zh, y, core):
        return zh * 8 + core * 4 + y

    def col_copy(n, to_z, h, s):
        return pltpu.make_async_remote_copy(
            total, cols.at[s], send_col.at[n], recv_col.at[h], device_id=(mine, ga_at(to_z, x)), device_id_type=MESH
        )

    my_col = col_slot(zh, y, core)
    lift = jnp.where(mine // 8 == zh, 2, 0)

    @pl.when(own)
    def _():
        cols[my_col] = total[...]

    for n, d in enumerate((0, 1, 3, 2)):
        to_z = rem(zl + lift + d, 4)

        @pl.when(jnp.logical_not(jnp.logical_and(own, to_z == zl)))
        def _():
            col_copy(n, to_z, zh * 2 + core, my_col).start()

    def row_copy(n, to_h, to_y, h, s):
        return pltpu.make_async_remote_copy(
            total, rows.at[s], send_row.at[n], recv_row.at[h],
            device_id=(pair_at(to_h, to_y, core), mine), device_id_type=MESH,
        )

    my_row = row_slot(zh, y, core)
    targets = [(h, d) for d in (2, 1, 3, 0) for h in range(2)]
    for n, (h, d) in enumerate(targets):
        row_copy(n, h, y + d, y * 2 + zh, my_row).start()

    def pass_col(n, d, slot, sem):
        two = cols.at[pl.ds(slot, 2)]
        return pltpu.make_async_remote_copy(
            two, two, send_fc.at[n], recv_fc.at[sem], device_id=(i, ga_at(zl, x + d)), device_id_type=MESH
        )

    def pass_row(h, c):
        four = rows.at[pl.ds(row_slot(h, 0, c), 4)]
        return pltpu.make_async_remote_copy(
            four, four, send_fr.at[h], recv_fr.at[h], device_id=(sibling, j), device_id_type=MESH
        )

    def wait_rows(h):
        for d in (0, 1, 3, 2):
            from_y = rem(y + d, 4)
            row_copy(0, h, from_y, from_y * 2 + h, row_slot(h, from_y, core)).wait_recv()
        pass_row(h, core).start()

    def wait_cols(step, h):
        for c in range(2):
            self_sent = jnp.logical_and(own, jnp.logical_and(h == zh, core == c))

            @pl.when(jnp.logical_not(self_sent))
            def _():
                col_copy(0, zl, h * 2 + c, col_slot(h, col_y, c)).wait_recv()

        for n, d in enumerate((2, 1, 3)):
            pass_col(step * 3 + n, d, col_slot(h, col_y, 0), col_y * 2 + h).start()

    halfs = (zh, 1 - zh)
    for step, h in enumerate(halfs):
        wait_cols(step, h)
        wait_rows(h)

    for copy in sent:
        copy.wait_send()
    for n, d in enumerate((0, 1, 3, 2)):
        to_z = rem(zl + lift + d, 4)

        @pl.when(jnp.logical_not(jnp.logical_and(own, to_z == zl)))
        def _():
            col_copy(n, to_z, zh * 2 + core, my_col).wait_send()

    for n, (h, d) in enumerate(targets):
        row_copy(n, h, y + d, y * 2 + zh, my_row).wait_send()

    for step, h in enumerate(halfs):
        pass_row(h, core).wait_send()
        pass_row(h, 1 - core).wait_recv()
        high, low = halves(jnp.concatenate([rows[h * 8 + c * 4 + y] for y in range(4) for c in range(2)], 0).T)
        turned = jnp.concatenate([high, high, low], 1)
        for n, d in enumerate((2, 1, 3)):
            pass_col(step * 3 + n, d, col_slot(h, col_y, 0), col_y * 2 + h).wait_send()
        for n, d in enumerate((1, 3, 2)):
            from_y = rem(col_y + d, 4)
            pass_col(0, d, col_slot(h, from_y, 0), from_y * 2 + h).wait_recv()
        blocks = -cols[pl.ds(h * 8, 8)]
        swapped = jnp.concatenate([-blocks[:, HERE:], blocks[:, :HERE]], 1)
        for o, value in enumerate((blocks, swapped)):
            high, low = halves(value.reshape(PAIRS, BLOCK))
            value = dot(turned, jnp.concatenate([high, low, high], 0))
            out[o] = value if step == 0 else out[o] + value


def coefficients(owner, pairs, energy_v, energy_c, sphere, orbitals):
    vmem = pl.BlockSpec(memory_space=pltpu.VMEM)
    hbm = pl.BlockSpec(memory_space=pl.ANY)
    points = NY * NZ
    dma = pltpu.SemaphoreType.DMA
    return pl.pallas_call(
        coefficients_kernel,
        out_shape=jax.ShapeDtypeStruct((2, BLOCK, BLOCK), jnp.float32),
        in_specs=[hbm] * 9,
        out_specs=vmem,
        scratch_shapes=[
            pltpu.SMEM((2, 8), jnp.int32),
            pltpu.SMEM((2, HERE), jnp.int32),
            pltpu.SMEM((8,), jnp.float32),
            pltpu.SMEM((8,), jnp.float32),
            pltpu.VMEM((1, NG), jnp.int32),
            pltpu.VMEM((16 * PLANES, points), jnp.bfloat16),
            pltpu.VMEM((WIDE, 256), jnp.bfloat16),
            pltpu.VMEM((2 * KY, 128), jnp.float32),
            pltpu.VMEM((4 * ROWS, 256), jnp.bfloat16),
            pltpu.VMEM((LOADS, 2 * CHUNKS // LOADS * ROWS, WIDE), jnp.bfloat16),
            pltpu.VMEM((CHUNKS, ROWS, 128), jnp.float32),
            pltpu.VMEM((GROUPS, 256 + 16, BLOCK), jnp.bfloat16),
            pltpu.VMEM((8 * ROWS, 256), jnp.bfloat16),
            pltpu.VMEM((GROUPS, 8, BLOCK), jnp.float32),
            pltpu.VMEM((GROUPS, 8, BLOCK), jnp.float32),
            pltpu.VMEM((8, BLOCK), jnp.float32),
            pltpu.VMEM((GROUPS, 8, BLOCK), jnp.float32),
            pltpu.VMEM((GROUPS, 8, BLOCK), jnp.float32),
            dma((LOADS + 8,)), dma((GROUPS,)), dma((GROUPS,)), dma((4,)), dma((4,)), dma((8,)), dma((8,)),
            dma((6,)), dma((8,)), dma((2,)), dma((2,)),
        ],
        compiler_params=pltpu.CompilerParams(
            collective_id=0, has_side_effects=True, vmem_limit_bytes=40 * 1024 * 1024
        ),
        name="coefficients",
    )(*[
        pltpu.with_memory_space_constraint(value, pltpu.HBM)
        for value in (
            owner, pairs.T, energy_v, energy_c, sphere.reshape(1, NG),
            orbitals.transpose(0, 2, 1, 3).reshape(16 * PLANES, points),
            jnp.asarray(table_along_z()), jnp.asarray(twiddles()), jnp.asarray(table_along_x()),
        )
    ])


def per_device(orbitals, owner, pair_list, valence_energy, conduction_energy, sphere_index):
    return coefficients(owner, pair_list, valence_energy, conduction_energy, sphere_index, orbitals)


def solution(mesh):
    return jax.shard_map(
        per_device,
        mesh=mesh,
        in_specs=(P(None, None, "ga", None), P(), P("pair", None), P(), P(), P()),
        out_specs=P(None, "ga", "pair"),
        check_vma=False,
    )
```

```python
import math

import jax
import jax.numpy as jnp
import ml_dtypes
import numpy as np
from jax import lax
from jax.experimental import pallas as pl
from jax.experimental.pallas import tpu as pltpu
from jax.sharding import PartitionSpec as P

NX = 96
NY = 96
NZ = 192
NG = 4096
PAIRS = 64
GROUPS = 16
PLANES = NX // GROUPS
HERE = PAIRS // GROUPS
ROWS = PLANES * HERE
STEP = 4
CHUNKS = NY // STEP
WIDE = STEP * NZ
KY = 8
KZ = 16
KX = 7
BLOCK = NG // GROUPS
LOADS = 4
MESH = pl.DeviceIdType.MESH
OFFSETS = sorted(((e, d) for e in range(4) for d in range(4)), key=lambda o: -(o[0] + min(o[1], 4 - o[1])))


def split(table):
    high = table.astype(ml_dtypes.bfloat16)
    low = (table - high.astype(np.float64)).astype(ml_dtypes.bfloat16)
    return high, low


def table_along_z():
    angle = 2 * math.pi * (np.arange(NZ)[:, None] * np.arange(KZ)[None, :] % NZ) / NZ
    table = np.zeros((STEP, NZ, STEP, 2, KZ))
    for r in range(STEP):
        table[r, :, r, 0] = np.cos(angle)
        table[r, :, r, 1] = -np.sin(angle)
    return np.concatenate(split(table.reshape(WIDE, STEP * 2 * KZ)), 1)


def twiddles():
    angle = 2 * math.pi * np.arange(KY)[:, None] * np.arange(STEP)[None, :] / NY
    angle = np.repeat(angle, 2 * KZ, 1)
    return np.concatenate([np.cos(angle), np.sin(angle)]).astype(np.float32)


def table_along_x():
    table = np.zeros((GROUPS, 2, PLANES, HERE, 256))
    for j in range(GROUPS):
        for x in range(PLANES):
            for f in range(-KX, KX + 1):
                angle = 2 * math.pi * (f * (PLANES * j + x) % NX) / NX
                table[j, 0, x, :, 16 + f + KX] = math.cos(angle)
                table[j, 1, x, :, 16 + f + KX] = math.sin(angle)
    high, low = split(table.reshape(GROUPS, 2 * ROWS, 256))
    return np.concatenate([high, low], 1)


def halves(value):
    high = value.astype(jnp.bfloat16)
    return high, (value - high.astype(jnp.float32)).astype(jnp.bfloat16)


def dot(left, right):
    return jnp.dot(left, right, preferred_element_type=jnp.float32)


def rem(value, size):
    return lax.rem(value, size)


def coefficients_kernel(
    owner_in, pairs_in, energy_v_in, energy_c_in, sphere_in, orbitals, table_z, table_y, table_x, out,
    owner, pairs, energy_v, energy_c, sphere, orb, tz, ty, tx, split_ref, along_z, hot, left, part, landed, total,
    rows, cols, sems, send1, recv1, send_col, recv_col, send_row, recv_row, send_fc, recv_fc, send_fr, recv_fr,
):
    i, j = lax.axis_index("pair"), lax.axis_index("ga")
    zh, y, core = i // 8, rem(i // 2, 4), rem(i, 2)
    zl, x = j // 4, rem(j, 4)
    sibling = i + 1 - 2 * core

    def pair_at(zh, y, core):
        return zh * 8 + rem(y, 4) * 2 + core

    def ga_at(zl, x):
        return rem(zl, 4) * 4 + rem(x, 4)

    mine = ga_at(zl + 2, x + 4 - y)
    own = mine == i
    col_y = rem(x + 4 - rem(i, 4), 4)

    moves = (
        (owner_in, owner), (pairs_in, pairs), (energy_v_in, energy_v), (energy_c_in, energy_c), (sphere_in, sphere),
        (table_z, tz.at[pl.ds(0, WIDE)]), (table_x.at[j], tx), (table_y, ty),
    )
    copies = [pltpu.make_async_copy(source, target, sems.at[LOADS + n]) for n, (source, target) in enumerate(moves)]
    loads = []
    span = CHUNKS // LOADS * WIDE
    for n in range(LOADS):
        lanes = pl.ds(n * span, span)
        loads.append(pltpu.make_async_copy(orbitals.at[:, lanes], orb.at[:, lanes], sems.at[n]))
    for copy in copies[4:5] + loads[:1] + copies[:4] + copies[5:6] + loads[1:] + copies[6:]:
        copy.start()

    barrier = pltpu.get_barrier_semaphore()

    def greet(device):
        pl.semaphore_signal(barrier, inc=1, device_id=device, device_id_type=MESH)

    turn = jnp.where(zl < 2, 1, 3)
    for e, d in OFFSETS[:-1]:
        greet((i, ga_at(zl + turn * e, x + d)))
    across = ga_at(jnp.where(zl < 2, 3, 0), x)
    for d in (2, 1, 3, 0):
        greet((pair_at(1 - zh, y + d, core), across))
    greet((pair_at(1 - zh, col_y, 1 - core), across))
    for d in (2, 1, 3):
        greet((pair_at(zh, y + d, core), j))
    greet((pair_at(zh, col_y, 1 - core), j))
    greet((sibling, j))
    side = jnp.where(rem(zl, 3) == 0, 1, 0)
    even = 1 - rem(x + 4 - (1 - core) + y, 2)
    greeted = (GROUPS - 1) + 4 + 8 * side + even * (2 + 4 * side)

    copies[4].wait()
    position = sphere[...]
    column = lax.shift_right_logical(lax.shift_right_logical(position, 6) * 43691, 17)
    index_z = position - column * NZ
    index_x = lax.shift_right_logical(lax.shift_right_logical(column, 5) * 43691, 17)
    index_y = column - index_x * NY
    freq_x = jnp.where(index_x >= NX // 2, index_x - NX, index_x)
    freq_y = jnp.where(index_y >= NY // 2, index_y - NY, index_y)
    freq_z = jnp.where(index_z >= NZ // 2, index_z - NZ, index_z)
    flip = freq_z < 0
    freq_x = jnp.where(flip, -freq_x, freq_x) + KX
    freq_y = jnp.where(flip, -freq_y, freq_y)
    mode = jnp.abs(freq_y) * 32 + jnp.where(freq_y < 0, 16, 0) + jnp.abs(freq_z)
    sign = jnp.where(flip, -1.0, 1.0)
    row = lax.broadcasted_iota(jnp.int32, (256, BLOCK), 0)
    for b in range(GROUPS):
        lanes = slice(b * BLOCK, (b + 1) * BLOCK)
        hot[b, :256] = jnp.where(row == mode[:, lanes], 1.0, 0.0).astype(jnp.bfloat16)
        hot[b, 16:32] = jnp.where(row[:16] == freq_x[:, lanes], 1.0, 0.0).astype(jnp.bfloat16)
        hot[b, 256:] = jnp.broadcast_to(sign[:, lanes], (16, BLOCK)).astype(jnp.bfloat16)

    for copy in copies[:4]:
        copy.wait()
    place = rem(lax.broadcasted_iota(jnp.int32, (8, WIDE), 0), HERE)
    slot_v = jnp.zeros((8, WIDE), jnp.int32)
    slot_c = jnp.zeros((8, WIDE), jnp.int32)
    gap = jnp.zeros((8, BLOCK), jnp.float32)
    for p in range(HERE):
        v, c = pairs[0, p], pairs[1, p]
        slot_v = jnp.where(place == p, owner[0, v], slot_v)
        slot_c = jnp.where(place == p, owner[1, c], slot_c)
        gap = jnp.where(place[:, :BLOCK] == p, energy_c[c] - energy_v[v], gap)
    scale = jnp.sqrt(2.0 / gap) * (1.0 / math.sqrt(NX * NY * NZ * math.sqrt(PAIRS)))

    upper = lax.broadcasted_iota(jnp.int32, (8, WIDE), 0) < HERE

    def pick(value, slots):
        return jnp.take_along_axis(value, slots, axis=0, mode="promise_in_bounds")

    copies[5].wait()
    tz[WIDE:] = tz[:WIDE]
    group = CHUNKS // LOADS
    for n in range(LOADS):
        loads[n].wait()

        @pl.loop(n * group // 2, (n + 1) * group // 2, unroll=True)
        def _(u):
            values = []
            for s in range(2):
                lanes = pl.ds(pl.multiple_of((2 * u + s) * WIDE, 128), WIDE)
                for a in range(PLANES // 2):
                    val = orb[16 * a : 16 * a + 16, lanes].astype(jnp.float32)
                    con = orb[48 + 16 * a : 64 + 16 * a, lanes].astype(jnp.float32)
                    first = pick(val[:8], slot_v) * pick(con[:8], slot_c)
                    second = pick(val[8:], slot_v) * pick(con[8:], slot_c)
                    values.append(jnp.where(upper, first, second))
            high, low = halves(jnp.concatenate(values, 0))
            here = pl.ds(pl.multiple_of(u * 2 * ROWS, 16), 2 * ROWS)
            split_ref[here, :WIDE] = high
            split_ref[here, WIDE:] = low

        here = slice(n * group * ROWS, (n + 1) * group * ROWS)
        result = dot(split_ref[here], tz[...])
        result = result[:, :128] + result[:, 128:]
        along_z[n * group : (n + 1) * group] = result.reshape(group, ROWS, 128)

    for copy in copies[6:]:
        copy.wait()
    lane = lax.broadcasted_iota(jnp.int32, (8, 128), 1)
    real_lane = rem(lane, 2 * KZ) < KZ
    turn_sign = jnp.where(real_lane, 1.0, -1.0)
    modes = [[], []]
    for a in range(ROWS // 8):
        here = slice(a * 8, a * 8 + 8)
        first, middle = along_z[0, here], along_z[CHUNKS // 2, here]
        even, odd = [], []
        for t in range(1, CHUNKS // 2):
            one, other = along_z[t, here], along_z[CHUNKS - t, here]
            even.append(one + other)
            odd.append(one - other)
        placed = [[None, None], [None, None]]
        for k in range(KY):
            total_cos = first + middle if k % 2 == 0 else first - middle
            total_sin = None
            for t in range(1, CHUNKS // 2):
                angle = 2 * math.pi * (k * t % CHUNKS) / CHUNKS
                total_cos = total_cos + even[t - 1] * math.cos(angle)
                term = odd[t - 1] * math.sin(angle)
                total_sin = term if total_sin is None else total_sin + term
            cosine, sine = ty[k : k + 1], ty[KY + k : KY + k + 1]
            same = cosine * total_cos - sine * total_sin
            cross = sine * total_cos + cosine * total_sin
            for shift in (2 * KZ, 4 * KZ):
                same = same + pltpu.roll(same, shift, 1)
                cross = cross + pltpu.roll(cross, shift, 1)
            cross = pltpu.roll(cross, KZ, 1) * turn_sign
            plus, minus = same + cross, same - cross
            real = jnp.where(real_lane, plus, pltpu.roll(minus, KZ, 1))
            imag = jnp.where(real_lane, pltpu.roll(plus, KZ, 1), minus)
            if k == 0:
                real, imag = jnp.where(real_lane, real, 0.0), jnp.where(real_lane, imag, 0.0)
            spot = lane // (2 * KZ) == k % 4
            for c, value in enumerate((real, imag)):
                old = placed[c][k // 4]
                placed[c][k // 4] = value if old is None else jnp.where(spot, value, old)
        for c in range(2):
            modes[c].append(jnp.concatenate(placed[c], 1))
    high, low = halves(jnp.concatenate(modes[0] + modes[1], 0))
    left[: 2 * ROWS] = high
    left[2 * ROWS : 4 * ROWS] = low
    left[4 * ROWS :] = tx[...]

    pl.semaphore_wait(barrier, greeted)
    upper = upper[:, :BLOCK]

    def to_group(n, slot, peer):
        return pltpu.make_async_remote_copy(
            part.at[n], landed.at[slot], send1.at[n], recv1.at[slot], device_id=(i, peer), device_id_type=MESH
        )

    sent = []
    for n, (e, d) in enumerate(OFFSETS):
        peer = ga_at(zl + turn * e, x + d)
        block = ga_at(zl + turn * e + 2, x + d + 4 - y)
        picked = dot(left[...], hot[block, :256])
        real = imag = jnp.zeros((8, BLOCK), jnp.float32)
        for a in range(ROWS // 8):
            re, im, cosine, sine = [
                picked[s * ROWS + a * 8 : s * ROWS + a * 8 + 8]
                + picked[s * ROWS + lag * ROWS + a * 8 : s * ROWS + lag * ROWS + a * 8 + 8]
                for s, lag in ((0, 2), (1, 2), (4, 2), (5, 2))
            ]
            real = real + cosine * re + sine * im
            imag = imag + cosine * im - sine * re
        imag = imag * hot[block, 256:].astype(jnp.float32)[:8]
        real = real + pltpu.roll(real, HERE, 0)
        imag = imag + pltpu.roll(imag, HERE, 0)
        part[n] = jnp.where(upper, real, imag) * scale
        if n < GROUPS - 1:
            copy = to_group(n, j, peer)
            copy.start()
            sent.append(copy)

    value = part[GROUPS - 1]
    for n, (e, d) in reversed(list(enumerate(OFFSETS[:-1]))):
        peer = ga_at(zl + turn * e, x + d)
        to_group(n, peer, peer).wait_recv()
        value = value + landed[peer]
    total[...] = value

    def col_slot(zh, y, core):
        return zh * 8 + y * 2 + core

    def row_slot(zh, y, core):
        return zh * 8 + core * 4 + y

    def col_copy(n, to_z, h, s):
        return pltpu.make_async_remote_copy(
            total, cols.at[s], send_col.at[n], recv_col.at[h], device_id=(mine, ga_at(to_z, x)), device_id_type=MESH
        )

    my_col = col_slot(zh, y, core)
    lift = jnp.where(mine // 8 == zh, 2, 0)

    @pl.when(own)
    def _():
        cols[my_col] = total[...]

    for n, d in enumerate((0, 1, 3, 2)):
        to_z = rem(zl + lift + d, 4)

        @pl.when(jnp.logical_not(jnp.logical_and(own, to_z == zl)))
        def _():
            col_copy(n, to_z, zh * 2 + core, my_col).start()

    def row_copy(n, to_h, to_y, h, s):
        return pltpu.make_async_remote_copy(
            total, rows.at[s], send_row.at[n], recv_row.at[h],
            device_id=(pair_at(to_h, to_y, core), mine), device_id_type=MESH,
        )

    my_row = row_slot(zh, y, core)
    targets = [(h, d) for d in (2, 1, 3, 0) for h in range(2)]
    for n, (h, d) in enumerate(targets):
        row_copy(n, h, y + d, y * 2 + zh, my_row).start()

    def pass_col(n, d, slot, sem):
        two = cols.at[pl.ds(slot, 2)]
        return pltpu.make_async_remote_copy(
            two, two, send_fc.at[n], recv_fc.at[sem], device_id=(i, ga_at(zl, x + d)), device_id_type=MESH
        )

    def pass_row(h, c):
        four = rows.at[pl.ds(row_slot(h, 0, c), 4)]
        return pltpu.make_async_remote_copy(
            four, four, send_fr.at[h], recv_fr.at[h], device_id=(sibling, j), device_id_type=MESH
        )

    def wait_rows(h):
        for d in (0, 1, 3, 2):
            from_y = rem(y + d, 4)
            row_copy(0, h, from_y, from_y * 2 + h, row_slot(h, from_y, core)).wait_recv()
        pass_row(h, core).start()

    def wait_cols(step, h):
        for c in range(2):
            self_sent = jnp.logical_and(own, jnp.logical_and(h == zh, core == c))

            @pl.when(jnp.logical_not(self_sent))
            def _():
                col_copy(0, zl, h * 2 + c, col_slot(h, col_y, c)).wait_recv()

        for n, d in enumerate((2, 1, 3)):
            pass_col(step * 3 + n, d, col_slot(h, col_y, 0), col_y * 2 + h).start()

    halfs = (zh, 1 - zh)
    for step, h in enumerate(halfs):
        wait_cols(step, h)
        wait_rows(h)

    for copy in sent:
        copy.wait_send()
    for n, d in enumerate((0, 1, 3, 2)):
        to_z = rem(zl + lift + d, 4)

        @pl.when(jnp.logical_not(jnp.logical_and(own, to_z == zl)))
        def _():
            col_copy(n, to_z, zh * 2 + core, my_col).wait_send()

    for n, (h, d) in enumerate(targets):
        row_copy(n, h, y + d, y * 2 + zh, my_row).wait_send()

    for step, h in enumerate(halfs):
        pass_row(h, core).wait_send()
        pass_row(h, 1 - core).wait_recv()
        high, low = halves(jnp.concatenate([rows[h * 8 + c * 4 + y] for y in range(4) for c in range(2)], 0).T)
        turned = jnp.concatenate([high, high, low], 1)
        for n, d in enumerate((2, 1, 3)):
            pass_col(step * 3 + n, d, col_slot(h, col_y, 0), col_y * 2 + h).wait_send()
        for n, d in enumerate((1, 3, 2)):
            from_y = rem(col_y + d, 4)
            pass_col(0, d, col_slot(h, from_y, 0), from_y * 2 + h).wait_recv()
        blocks = -cols[pl.ds(h * 8, 8)]
        swapped = jnp.concatenate([-blocks[:, HERE:], blocks[:, :HERE]], 1)
        for o, value in enumerate((blocks, swapped)):
            high, low = halves(value.reshape(PAIRS, BLOCK))
            value = dot(turned, jnp.concatenate([high, low, high], 0))
            out[o] = value if step == 0 else out[o] + value


def coefficients(owner, pairs, energy_v, energy_c, sphere, orbitals):
    vmem = pl.BlockSpec(memory_space=pltpu.VMEM)
    hbm = pl.BlockSpec(memory_space=pl.ANY)
    points = NY * NZ
    dma = pltpu.SemaphoreType.DMA
    return pl.pallas_call(
        coefficients_kernel,
        out_shape=jax.ShapeDtypeStruct((2, BLOCK, BLOCK), jnp.float32),
        in_specs=[hbm] * 9,
        out_specs=vmem,
        scratch_shapes=[
            pltpu.SMEM((2, 8), jnp.int32),
            pltpu.SMEM((2, HERE), jnp.int32),
            pltpu.SMEM((8,), jnp.float32),
            pltpu.SMEM((8,), jnp.float32),
            pltpu.VMEM((1, NG), jnp.int32),
            pltpu.VMEM((16 * PLANES, points), jnp.bfloat16),
            pltpu.VMEM((2 * WIDE, 256), jnp.bfloat16),
            pltpu.VMEM((2 * KY, 128), jnp.float32),
            pltpu.VMEM((4 * ROWS, 256), jnp.bfloat16),
            pltpu.VMEM((CHUNKS * ROWS, 2 * WIDE), jnp.bfloat16),
            pltpu.VMEM((CHUNKS, ROWS, 128), jnp.float32),
            pltpu.VMEM((GROUPS, 256 + 16, BLOCK), jnp.bfloat16),
            pltpu.VMEM((8 * ROWS, 256), jnp.bfloat16),
            pltpu.VMEM((GROUPS, 8, BLOCK), jnp.float32),
            pltpu.VMEM((GROUPS, 8, BLOCK), jnp.float32),
            pltpu.VMEM((8, BLOCK), jnp.float32),
            pltpu.VMEM((GROUPS, 8, BLOCK), jnp.float32),
            pltpu.VMEM((GROUPS, 8, BLOCK), jnp.float32),
            dma((LOADS + 8,)), dma((GROUPS,)), dma((GROUPS,)), dma((4,)), dma((4,)), dma((8,)), dma((8,)),
            dma((6,)), dma((8,)), dma((2,)), dma((2,)),
        ],
        compiler_params=pltpu.CompilerParams(
            collective_id=0, has_side_effects=True, vmem_limit_bytes=40 * 1024 * 1024
        ),
        name="coefficients",
    )(*[
        pltpu.with_memory_space_constraint(value, pltpu.HBM)
        for value in (
            owner, pairs.T, energy_v, energy_c, sphere.reshape(1, NG),
            orbitals.transpose(0, 2, 1, 3).reshape(16 * PLANES, points),
            jnp.asarray(table_along_z()), jnp.asarray(twiddles()), jnp.asarray(table_along_x()),
        )
    ])


def per_device(orbitals, owner, pair_list, valence_energy, conduction_energy, sphere_index):
    return coefficients(owner, pair_list, valence_energy, conduction_energy, sphere_index, orbitals)


def solution(mesh):
    return jax.shard_map(
        per_device,
        mesh=mesh,
        in_specs=(P(None, None, "ga", None), P(), P("pair", None), P(), P(), P()),
        out_specs=P(None, "ga", "pair"),
        check_vma=False,
    )
```
